512 devices in a mesh: ctx: 64 (over z, y), head: 8 (over x, core).
Axes of the slice: x: 4, y: 8, z: 8, core: 2. Of those that a mesh axis runs over, the one named last changes fastest.
Arguments:
- queries: bfloat16 [2, 64, 16384], P(None, 'ctx', 'head'), may hold values from -6 to 6
- prompt_keys: bfloat16 [32768, 1024], P('ctx', 'head'), may hold values from -6 to 6
- prompt_values: bfloat16 [32768, 1024], P('ctx', 'head'), may hold values from -6 to 6
- selected: int32 [64, 8, 512], P(None, 'head', 'ctx'), may hold values from -1 to 7, as said below
- cache_keys: bfloat16 [64, 256, 1024], P('ctx', None, 'head'), may hold values from -6 to 6
- cache_values: bfloat16 [64, 256, 1024], P('ctx', None, 'head'), may hold values from -6 to 6
- new_keys: bfloat16 [2, 64, 1024], P(None, 'ctx', 'head'), may hold values from -6 to 6
- new_values: bfloat16 [2, 64, 1024], P(None, 'ctx', 'head'), may hold values from -6 to 6
- positions: int32 [64], P('ctx'), may hold values from 1 to 256, as said below
- out_weight: bfloat16 [16384, 16384], P('head', 'ctx'), may hold values from -0.375 to 0.375
Outputs:
- mixed: bfloat16 [2, 64, 16384], P(None, 'head', 'ctx')
The draws below stay inside these ranges and needn't reach their ends.
Inputs may be any that keep to these rules, and one draw needn't show every extreme that they name: `selected`: entry [r, g, k * 8 + i] is the i-th block that sample r selects for key-value head g on context shard k, numbered within the shard; a sample's blocks on one shard are distinct, and -1 marks unused slots, which follow the used ones. Some sample fills all 8 slots of some shard. `positions`: some sample has 256 cached tokens.
All inputs are finite; a program needn't handle non-finite values.
Results may differ from the reference program's by a relative error of at most 0.005.
Values may be sent and summed in bfloat16 or wider, within the bound.
No kernel may reach another device: no remote copies, remote signals or barrier semaphores. Data moves between devices by JAX's collectives and lax.ppermute only.
A program may use at most 64 MiB of HBM per device.

```python
import functools
import math
import jax
import jax.numpy as jnp
from jax import lax

D = 16384
H = 128
KVH = 8
HD = 128
ROWS = 64
CTX_DEV = 512
GEN = 256
BLOCK = 64
SEL_DEV = 8
PROMPT = 32768
SELECT = 512
N_CTX = 64


def shared_direction(key):
    key = jax.random.fold_in(key, 202)
    return jax.random.normal(key, (2, ROWS, KVH, HD), jnp.float32)


def draw_queries(key, part):
    base_key = key
    key = jax.random.fold_in(key, 1)
    direction = shared_direction(base_key)[:, :, :, None, :]
    noise = jax.random.normal(key, (2, ROWS, KVH, H // KVH, HD), jnp.float32)
    sample = jnp.clip(0.45 * direction + 0.89 * noise, -6.0, 6.0).reshape(2, ROWS, H * HD)
    return sample.astype(jnp.bfloat16)


def draw_prompt_keys(key, part):
    key = jax.random.fold_in(key, 6)
    sample = jnp.clip(jax.random.normal(key, (PROMPT, KVH * HD), jnp.float32), -6.0, 6.0)
    return sample.astype(jnp.bfloat16)


def draw_cache_keys(key, part):
    key = jax.random.fold_in(key, 2)
    sample = jnp.clip(3.0 * jax.random.normal(key, (ROWS, GEN, KVH * HD), jnp.float32), -6.0, 6.0)
    return sample.astype(jnp.bfloat16)


def draw_new_keys(key, part):
    base_key = key
    key = jax.random.fold_in(key, 3)
    direction = shared_direction(base_key).reshape(2, ROWS, KVH * HD)
    noise = jax.random.normal(key, (2, ROWS, KVH * HD), jnp.float32)
    sample = jnp.clip(1.6 * direction + 0.5 * noise, -6.0, 6.0)
    return sample.astype(jnp.bfloat16)


def draw_selected(key, part):
    key = jax.random.fold_in(key, 4)
    key_heat, key_want, key_row, key_group, key_shard, key_order = jax.random.split(key, 6)
    shard_total = SELECT // SEL_DEV
    block_count = CTX_DEV // BLOCK
    shard_heat = jax.random.randint(key_heat, (1, KVH, shard_total), 0, 4)
    wanted = jax.random.randint(key_want, (ROWS, KVH, shard_total), 0, SEL_DEV * shard_heat // 2 + 1)
    counts = jnp.minimum(wanted, SEL_DEV)
    row_pick = jax.random.randint(key_row, (), 0, ROWS)
    group_pick = jax.random.randint(key_group, (), 0, KVH)
    shard_pick = jax.random.randint(key_shard, (), 0, shard_total)
    counts = counts.at[row_pick, group_pick, shard_pick].set(SEL_DEV)
    ranking = jax.random.randint(key_order, (ROWS, KVH, shard_total, block_count), 0, 1 << 20) * block_count
    ranking = ranking + jnp.arange(block_count, dtype=jnp.int32)
    picked = jnp.argsort(ranking, axis=-1)[..., :SEL_DEV].astype(jnp.int32)
    slot_index = jnp.arange(SEL_DEV, dtype=jnp.int32)
    chosen = jnp.where(slot_index < counts[..., None], picked, -1)
    return chosen.reshape(ROWS, KVH, SELECT).astype(jnp.int32)


def draw_positions(key, part):
    key = jax.random.fold_in(key, 5)
    key_len, key_row = jax.random.split(key)
    lengths = jax.random.randint(key_len, (ROWS,), 1, GEN + 1)
    row_pick = jax.random.randint(key_row, (), 0, ROWS)
    return lengths.at[row_pick].set(GEN).astype(jnp.int32)


def block_scale(key, shape, shards, low, top_value):
    loudness = 1.0
    for dim, blocks in shards:
        heights = jax.random.uniform(jax.random.fold_in(jax.random.fold_in(key, 6), dim), (blocks,), jnp.float32, low / len(shards), top_value / len(shards))
        loudness = loudness * jnp.repeat(jnp.exp(heights), shape[dim] // blocks).reshape((-1,) + (1,) * (len(shape) - 1 - dim))
    return loudness


def normal_values(key, dims, scale, most, shards=(), kind=jnp.bfloat16):
    factor_of = block_scale(key, dims, shards, -0.22, 0.18) if shards else 1.0
    result = jax.random.normal(key, dims, jnp.float32) * scale * factor_of
    return jnp.minimum(jnp.maximum(result, -most), most).astype(kind)


def setup_inputs(seed: int = 0) -> dict:
    key_list = jax.random.split(jax.random.key(seed), 11)
    return {
        "queries": draw_queries(jax.random.fold_in(key_list[10], 71), 0),
        "prompt_keys": draw_prompt_keys(jax.random.fold_in(key_list[10], 71), 0),
        "prompt_values": normal_values(key_list[2], (PROMPT, KVH * HD), 1.0, 6.0, ((0, 64), (1, 8))),
        "selected": draw_selected(jax.random.fold_in(key_list[10], 71), 0),
        "cache_keys": draw_cache_keys(jax.random.fold_in(key_list[10], 71), 0),
        "cache_values": normal_values(key_list[5], (ROWS, GEN, KVH * HD), 1.0, 6.0, ((0, 64), (2, 8))),
        "new_keys": draw_new_keys(jax.random.fold_in(key_list[10], 71), 0),
        "new_values": normal_values(key_list[7], (2, ROWS, KVH * HD), 1.0, 6.0, ((1, 64), (2, 8))),
        "positions": draw_positions(jax.random.fold_in(key_list[10], 71), 0),
        "out_weight": normal_values(key_list[9], (H * HD, D), (H * HD // 64) ** -0.5, 0.375, ((0, 8), (1, 64))),
    }


NEGATIVE = -1e+30

def own_partial(query_rows, cache_keys, cache_values, new_keys, new_values, positions):
    step_count, row_count, group_count, per_group, head_dim = query_rows.shape
    score_scale = 1.0 / math.sqrt(head_dim)
    slot_total = cache_keys.shape[1]
    new_total = new_keys.shape[0]
    query_float = query_rows.astype(jnp.float32)
    cache_key_float = cache_keys.reshape(row_count, slot_total, group_count, head_dim).astype(jnp.float32)
    cache_value_float = cache_values.reshape(row_count, slot_total, group_count, head_dim).astype(jnp.float32)
    new_key_float = new_keys.reshape(new_total, row_count, group_count, head_dim).astype(jnp.float32)
    new_value_float = new_values.reshape(new_total, row_count, group_count, head_dim).astype(jnp.float32)
    cache_scores = jnp.einsum('srgqd,rjgd->srgqj', query_float, cache_key_float) * score_scale
    new_scores = jnp.einsum('srgqd,trgd->srgqt', query_float, new_key_float) * score_scale
    cache_alive = (jnp.arange(slot_total, dtype=jnp.int32)[None, :] < positions[:, None])[None, :, None, None, :]
    new_alive = (jnp.arange(new_total, dtype=jnp.int32)[None, :] <= jnp.arange(step_count, dtype=jnp.int32)[:, None])[:, None, None, None, :]
    top_score = jnp.maximum(lax.optimization_barrier(jnp.max(jnp.where(cache_alive, cache_scores, NEGATIVE), axis=-1)), lax.optimization_barrier(jnp.max(jnp.where(new_alive, new_scores, NEGATIVE), axis=-1)))
    cache_weights = jnp.where(cache_alive, jnp.exp(cache_scores - top_score[..., None]), 0.0)
    new_weights = jnp.where(new_alive, jnp.exp(new_scores - top_score[..., None]), 0.0)
    mass_sum = lax.optimization_barrier(jnp.sum(cache_weights, axis=-1)) + lax.optimization_barrier(jnp.sum(new_weights, axis=-1))
    output = jnp.einsum('srgqj,rjgd->srgqd', cache_weights.astype(jnp.bfloat16).astype(jnp.float32), cache_value_float)
    output = output + jnp.einsum('srgqt,trgd->srgqd', new_weights.astype(jnp.bfloat16).astype(jnp.float32), new_value_float)
    return (output, top_score, mass_sum)

def shard_partial(query_group, shard_inputs):
    key_blocks, value_blocks, chosen = shard_inputs
    alive = chosen >= 0
    safe_ids = jnp.maximum(chosen, 0).astype(jnp.int32)
    key_rows = key_blocks[safe_ids].astype(jnp.float32)
    value_rows = value_blocks[safe_ids].astype(jnp.float32)
    score_scale = 1.0 / math.sqrt(query_group.shape[-1])
    scores = jnp.einsum('srqd,rkbd->srqkb', query_group, key_rows) * score_scale
    alive_mask = alive[None, :, None, :, None]
    top_score = lax.optimization_barrier(jnp.max(jnp.where(alive_mask, scores, NEGATIVE), axis=(-2, -1)))
    weights = jnp.where(alive_mask, jnp.exp(scores - top_score[..., None, None]), 0.0)
    mass_sum = lax.optimization_barrier(jnp.sum(weights, axis=(-2, -1)))
    output = jnp.einsum('srqkb,rkbd->srqd', weights.astype(jnp.bfloat16).astype(jnp.float32), value_rows)
    return (output, top_score, mass_sum)

def reference(queries, prompt_keys, prompt_values, selected, cache_keys, cache_values, new_keys, new_values, positions, out_weight):
    step_count = queries.shape[0]
    per_group = H // KVH
    block_count = CTX_DEV // BLOCK
    query_rows = queries.reshape(step_count, ROWS, KVH, per_group, HD)
    key_blocks = prompt_keys.reshape(N_CTX, block_count, BLOCK, KVH, HD)
    value_blocks = prompt_values.reshape(N_CTX, block_count, BLOCK, KVH, HD)
    chosen = selected.reshape(ROWS, KVH, N_CTX, SEL_DEV)
    own_out, own_top, own_mass = own_partial(query_rows, cache_keys, cache_values, new_keys, new_values, positions)
    groups_out = []
    for group_index in range(KVH):
        query_group = query_rows[:, :, group_index].astype(jnp.float32)
        shard_inputs = (key_blocks[:, :, :, group_index], value_blocks[:, :, :, group_index], jnp.moveaxis(chosen[:, group_index], 1, 0))
        part_out, part_top, part_mass = lax.map(functools.partial(shard_partial, query_group), shard_inputs)
        shard_top = lax.optimization_barrier(jnp.max(part_top, axis=0))
        factor = jnp.exp(part_top - shard_top[None])
        shard_mass = lax.optimization_barrier(jnp.sum(factor * part_mass, axis=0))
        shard_sum = lax.optimization_barrier(jnp.sum(factor[..., None] * part_out, axis=0))
        group_top = own_top[:, :, group_index]
        best_score = jnp.maximum(shard_top, group_top)
        shard_factor = jnp.exp(shard_top - best_score)
        own_factor = jnp.exp(group_top - best_score)
        numer = shard_sum * shard_factor[..., None] + own_out[:, :, group_index] * own_factor[..., None]
        denom = shard_mass * shard_factor + own_mass[:, :, group_index] * own_factor
        groups_out.append((numer / denom[..., None]).astype(jnp.bfloat16))
    attended = jnp.stack(groups_out, axis=2).reshape(step_count * ROWS, H * HD)
    mixed = jnp.dot(attended, out_weight, preferred_element_type=jnp.float32).astype(jnp.bfloat16)
    return mixed.reshape(step_count, ROWS, D)
```

```python
import math

import jax
import jax.numpy as jnp
from jax import lax
from jax.experimental import pallas as pl
from jax.experimental.pallas import tpu as pltpu
from jax.sharding import PartitionSpec as P

HD = 128
PER = 16
BLOCK = 64
STEPS = 2
ITEM = STEPS * PER
STAT = 8
NEGATIVE = -1e30
SCALE = math.log2(math.e) / math.sqrt(HD)
TILE = 8

VMEM = pl.BlockSpec(memory_space=pltpu.VMEM)
SMEM = pl.BlockSpec(memory_space=pltpu.SMEM)
PARAMS = pltpu.CompilerParams(vmem_limit_bytes=24 * 1024 * 1024)
F32 = jnp.float32
BF16 = jnp.bfloat16


def dot(a, b):
    return lax.dot_general(a, b, (((1,), (0,)), ((), ())), preferred_element_type=F32)


def dot_t(a, b):
    return lax.dot_general(a, b, (((1,), (1,)), ((), ())), preferred_element_type=F32)


def iota(shape, dim):
    return lax.broadcasted_iota(jnp.int32, shape, dim)


def item_rows(q_ref, rows_ref):
    whole = q_ref[...].astype(F32)
    for step in range(STEPS):
        for head in range(PER):
            row = step * PER + head
            rows_ref[row : row + 1, :] = whole[step : step + 1, head * HD : (head + 1) * HD]
    return rows_ref[...]


def to_lanes(column, count):
    shape = (count, ITEM, HD)
    pick = iota(shape, 1) == iota(shape, 2) % ITEM
    return jnp.sum(jnp.where(pick, column.reshape(shape), 0.0), axis=1)


def spread_kernel(q_ref, out_ref, rows_ref):
    rows = item_rows(q_ref, rows_ref).astype(BF16)
    out_ref[...] = jnp.broadcast_to(rows[None], out_ref.shape)


def own_kernel(
    q_ref, sel_ref, ck_ref, cv_ref, nk_ref, nv_ref, pos_ref, bias_ref, out_ref, log_ref, rows_ref
):
    rows = item_rows(q_ref, rows_ref)
    slots = ck_ref.shape[0]
    scores = dot_t(rows.astype(BF16), ck_ref[...]) * SCALE
    alive = iota((ITEM, slots), 1) < pos_ref[0]
    scores = jnp.where(alive, scores, NEGATIVE)
    top = jnp.max(scores, axis=1, keepdims=True)
    step = iota((ITEM, 1), 0) // PER
    new_scores = []
    for token in range(STEPS):
        key = nk_ref[token : token + 1, :].astype(F32)
        score = jnp.sum(rows * key, axis=1, keepdims=True) * SCALE
        score = jnp.where(step >= token, score, NEGATIVE)
        new_scores.append(score)
        top = jnp.maximum(top, score)
    weights = jnp.where(alive, jnp.exp2(scores - top), 0.0)
    mass = jnp.sum(weights, axis=1, keepdims=True)
    total = dot(weights.astype(BF16), cv_ref[...])
    for token in range(STEPS):
        weight = jnp.where(step >= token, jnp.exp2(new_scores[token] - top), 0.0)
        mass = mass + weight
        value = nv_ref[token : token + 1, :].astype(F32)
        total = total + weight.astype(BF16).astype(F32) * value
    out_ref[...] = total / mass
    log_mass = jnp.broadcast_to(top + jnp.log2(mass), (ITEM, HD))
    log_ref[...] = jnp.broadcast_to(to_lanes(log_mass, 1), log_ref.shape)
    slot_count, samples = sel_ref.shape
    tokens = bias_ref.shape[1]
    blocks = tokens // BLOCK
    number = iota((blocks, samples), 0)
    chosen = jnp.zeros((blocks, samples), F32)
    for slot in range(slot_count):
        chosen = jnp.where(sel_ref[slot : slot + 1, :] == number, 1.0, chosen)
    widen = (iota((blocks, tokens), 1) // BLOCK == iota((blocks, tokens), 0)).astype(F32)
    hit = lax.dot_general(chosen, widen, (((0,), (0,)), ((), ())), preferred_element_type=F32)
    bias_ref[...] = jnp.where(hit > 0.5, 0.0, NEGATIVE)


def prompt_kernel(q_ref, k_ref, v_ref, bias_ref, out_ref):
    samples = q_ref.shape[0]
    tokens = k_ref.shape[0]
    keys = k_ref[...]
    values = jnp.concatenate([v_ref[...], jnp.ones((tokens, HD), BF16)], axis=1)
    for first in range(0, samples, TILE):
        here = slice(first, first + TILE)
        q = q_ref[here].reshape(TILE * ITEM, HD)
        scores = dot_t(q, keys) * SCALE
        scores = scores.reshape(TILE, ITEM, tokens) + bias_ref[here][:, None, :]
        scores = scores.reshape(TILE * ITEM, tokens)
        top = jnp.max(scores, axis=1, keepdims=True)
        weights = jnp.exp2(scores - top).astype(BF16)
        total = dot(weights, values)
        mass = total[:, HD:]
        out_ref[here, :ITEM, :] = (total[:, :HD] / mass).astype(BF16).reshape(TILE, ITEM, HD)
        log_mass = to_lanes(top + jnp.log2(mass), TILE)
        high = log_mass.astype(BF16).astype(F32)
        rest = log_mass - high
        middle = rest.astype(BF16).astype(F32)
        low = rest - middle
        shape = (TILE, STAT, HD)
        row = iota(shape, 1)
        stat = jnp.where(row == 0, jnp.broadcast_to(high[:, None, :], shape), 0.0)
        stat = jnp.where(row == 1, jnp.broadcast_to(middle[:, None, :], shape), stat)
        stat = jnp.where(row == 2, jnp.broadcast_to(low[:, None, :], shape), stat)
        out_ref[here, ITEM:, :] = stat.astype(BF16)


def combine_kernel(part_ref, own_ref, own_log_ref, out_ref):
    shards = part_ref.shape[0]
    log_mass = jnp.sum(part_ref[:, ITEM:, :].astype(F32), axis=1)
    own_log = own_log_ref[0:1, :]
    best = jnp.maximum(jnp.max(log_mass, axis=0, keepdims=True), own_log)
    weights = jnp.exp2(log_mass - best)
    own_weight = jnp.exp2(own_log - best)
    whole = jnp.sum(weights, axis=0, keepdims=True) + own_weight
    weights = weights / whole
    own_weight = own_weight / whole
    per_lane = HD // ITEM
    groups = shards // per_lane
    lane = iota((groups, HD), 1) // ITEM
    packed = jnp.zeros((groups, HD), F32)
    for turn in range(per_lane):
        packed = jnp.where(lane == turn, weights[turn * groups : (turn + 1) * groups], packed)
    pick = iota((ITEM, HD), 0) == iota((ITEM, HD), 1) % ITEM
    factors = []
    rows = []
    for group in range(groups):
        factors.append(jnp.where(pick, packed[group : group + 1], 0.0))
        for turn in range(per_lane):
            rows.append(part_ref[group + turn * groups, :ITEM, :])
    factor = jnp.concatenate(factors, axis=1)
    high = factor.astype(BF16)
    low = (factor - high.astype(F32)).astype(BF16)
    total = dot(jnp.concatenate([high, low], axis=0), jnp.concatenate(rows, axis=0))
    total = total[:ITEM] + total[ITEM:]
    own_column = jnp.sum(
        jnp.where(iota((ITEM, HD), 0) == iota((ITEM, HD), 1), own_weight, 0.0),
        axis=1,
        keepdims=True,
    )
    attended = (total + own_column * own_ref[...]).astype(BF16)
    out_ref[...] = jnp.broadcast_to(attended[None], out_ref.shape)


def project_kernel(x_ref, w_ref, out_ref, rows_ref):
    samples = x_ref.shape[0]
    parts = out_ref.shape[0]
    per_part = samples // parts
    rows_ref[...] = x_ref[...].reshape(samples * ITEM, HD).astype(F32)
    columns = []
    for head in range(PER):
        pieces = [
            rows_ref[pl.ds(step * PER + head, samples, stride=ITEM), :] for step in range(STEPS)
        ]
        columns.append(jnp.concatenate(pieces, axis=0).astype(BF16))
    product = dot(jnp.concatenate(columns, axis=1), w_ref[...])
    for part in range(parts):
        pieces = [
            product[step * samples + part * per_part : step * samples + (part + 1) * per_part]
            for step in range(STEPS)
        ]
        out_ref[part] = jnp.concatenate(pieces, axis=0).astype(out_ref.dtype)


def sum_kernel(x_ref, out_ref):
    total = jnp.sum(x_ref[...].astype(F32), axis=0)
    out_ref[...] = total.reshape(out_ref.shape).astype(BF16)


def call(kernel, name, out_shape, in_specs, out_specs, scratch=(), flops=0, moved=0):
    return pl.pallas_call(
        kernel,
        name=name,
        out_shape=out_shape,
        in_specs=in_specs,
        out_specs=out_specs,
        scratch_shapes=scratch,
        compiler_params=PARAMS,
        cost_estimate=pl.CostEstimate(flops=flops, bytes_accessed=moved, transcendentals=0),
    )


def swap(array, axis):
    return lax.all_to_all(array, axis, split_axis=0, concat_axis=0, tiled=True)


def shards(
    queries,
    prompt_keys,
    prompt_values,
    selected,
    cache_keys,
    cache_values,
    new_keys,
    new_values,
    positions,
    out_weight,
):
    samples = lax.axis_size("ctx")
    parts = lax.axis_size("head")
    tokens = prompt_keys.shape[0]
    columns = out_weight.shape[1]
    struct = jax.ShapeDtypeStruct
    rows_scratch = pltpu.VMEM((ITEM, HD), F32)
    q = queries.reshape(STEPS, PER * HD)
    spread = call(
        spread_kernel, "spread", struct((samples, ITEM, HD), BF16), [VMEM], VMEM, [rows_scratch]
    )(q)
    gathered = swap(spread, "ctx")
    bias, own, own_log = call(
        own_kernel,
        "own",
        (struct((samples, tokens), F32), struct((ITEM, HD), F32), struct((8, HD), F32)),
        [VMEM] * 6 + [SMEM],
        (VMEM, VMEM, VMEM),
        [rows_scratch],
        flops=10**6,
        moved=3 * 10**5,
    )(
        q,
        selected[:, 0, :].T,
        cache_keys[0],
        cache_values[0],
        new_keys[:, 0],
        new_values[:, 0],
        positions,
    )
    parts_out = call(
        prompt_kernel,
        "prompt",
        struct((samples, ITEM + STAT, HD), BF16),
        [VMEM] * 4,
        VMEM,
    )(gathered, prompt_keys, prompt_values, bias)
    received = swap(parts_out, "ctx")
    attended = call(
        combine_kernel, "combine", struct((samples, ITEM, HD), BF16), [VMEM] * 3, VMEM
    )(received, own, own_log)
    every = swap(attended, "ctx")
    product = call(
        project_kernel,
        "project",
        struct((parts, STEPS * samples // parts, columns), F32),
        [VMEM] * 2,
        VMEM,
        [pltpu.VMEM((samples * ITEM, HD), F32)],
    )(every, out_weight)
    terms = swap(product, "head")
    return call(
        sum_kernel, "sum", struct((STEPS, samples // parts, columns), BF16), [VMEM], VMEM
    )(terms)


def solution(mesh):
    placed = (
        P(None, "ctx", "head"),
        P("ctx", "head"),
        P("ctx", "head"),
        P(None, "head", "ctx"),
        P("ctx", None, "head"),
        P("ctx", None, "head"),
        P(None, "ctx", "head"),
        P(None, "ctx", "head"),
        P("ctx"),
        P("head", "ctx"),
    )
    return jax.shard_map(
        shards, mesh=mesh, in_specs=placed, out_specs=P(None, "head", "ctx"), check_vma=False
    )
```

```python
import math

import jax
import jax.numpy as jnp
from jax import lax
from jax.experimental import pallas as pl
from jax.experimental.pallas import tpu as pltpu
from jax.sharding import Mesh
from jax.sharding import PartitionSpec as P

HD = 128
PER = 16
BLOCK = 64
STEPS = 2
HALVES = 2
HALF = PER // HALVES
PART = STEPS * HALF
ITEM = HALVES * PART
STAT = 8
FLAG = 16
NEGATIVE = -1e30
SCALE = math.log2(math.e) / math.sqrt(HD)
TILE = 8
SAMPLES = ("zh", "zl", "yh")

VMEM = pl.BlockSpec(memory_space=pltpu.VMEM)
SMEM = pl.BlockSpec(memory_space=pltpu.SMEM)
PARAMS = pltpu.CompilerParams(vmem_limit_bytes=24 * 1024 * 1024)
F32 = jnp.float32
BF16 = jnp.bfloat16


def dot(a, b):
    return lax.dot_general(a, b, (((1,), (0,)), ((), ())), preferred_element_type=F32)


def dot_t(a, b):
    return lax.dot_general(a, b, (((1,), (1,)), ((), ())), preferred_element_type=F32)


def iota(shape, dim):
    return lax.broadcasted_iota(jnp.int32, shape, dim)


def item_rows(q_ref, rows_ref):
    whole = q_ref[...].astype(F32)
    for step in range(STEPS):
        for head in range(PER):
            row = head // HALF * PART + step * HALF + head % HALF
            rows_ref[row : row + 1, :] = whole[step : step + 1, head * HD : (head + 1) * HD]
    return rows_ref[...]


def spread_kernel(q_ref, out_ref, rows_ref):
    rows = item_rows(q_ref, rows_ref).astype(BF16)
    out_ref[...] = jnp.broadcast_to(rows[None], out_ref.shape)


def pack_kernel(k_ref, v_ref, sel_ref, out_ref):
    tokens = k_ref.shape[0]
    out_ref[:tokens, :] = k_ref[...]
    out_ref[tokens : 2 * tokens, :] = v_ref[...]
    slots, samples = sel_ref.shape
    number = iota((FLAG, samples), 0)
    chosen = jnp.zeros((FLAG, samples), F32)
    for slot in range(slots):
        chosen = jnp.where(sel_ref[slot : slot + 1, :] == number, 1.0, chosen)
    chosen = jnp.concatenate([chosen, jnp.zeros((FLAG, HD - samples), F32)], axis=1)
    out_ref[2 * tokens :, :] = chosen.astype(BF16)


def own_kernel(q_ref, ck_ref, cv_ref, nk_ref, nv_ref, pos_ref, out_ref, log_ref, rows_ref):
    rows = item_rows(q_ref, rows_ref)
    slots = ck_ref.shape[0]
    scores = dot_t(rows.astype(BF16), ck_ref[...]) * SCALE
    alive = iota((ITEM, slots), 1) < pos_ref[0]
    scores = jnp.where(alive, scores, NEGATIVE)
    top = jnp.max(scores, axis=1, keepdims=True)
    step = iota((ITEM, 1), 0) // HALF % STEPS
    new_scores = []
    for token in range(STEPS):
        key = nk_ref[token : token + 1, :].astype(F32)
        score = jnp.sum(rows * key, axis=1, keepdims=True) * SCALE
        score = jnp.where(step >= token, score, NEGATIVE)
        new_scores.append(score)
        top = jnp.maximum(top, score)
    weights = jnp.where(alive, jnp.exp2(scores - top), 0.0)
    mass = jnp.sum(weights, axis=1, keepdims=True)
    total = dot(weights.astype(BF16), cv_ref[...])
    for token in range(STEPS):
        weight = jnp.where(step >= token, jnp.exp2(new_scores[token] - top), 0.0)
        mass = mass + weight
        value = nv_ref[token : token + 1, :].astype(F32)
        total = total + weight.astype(BF16).astype(F32) * value
    out_ref[...] = total / mass
    log_ref[...] = jnp.broadcast_to(top + jnp.log2(mass), (ITEM, HD))


def bias_of(pack_ref, yl, samples, tokens):
    flags = pack_ref[2 * tokens :, :]
    mine = (iota((samples, HD), 1) == 2 * iota((samples, HD), 0) + yl).astype(BF16)
    chosen = dot_t(mine, flags).astype(BF16)
    widen = iota((FLAG, tokens), 1) // BLOCK == iota((FLAG, tokens), 0)
    hit = dot(chosen, widen.astype(BF16))
    return jnp.where(hit > 0.5, 0.0, NEGATIVE)


def prompt_kernel(
    place_ref, q_ref, here_ref, there_ref, own_ref, own_log_ref, out_ref, total_ref, log_ref
):
    samples = q_ref.shape[0]
    tokens = (here_ref.shape[0] - FLAG) // 2
    packs = (here_ref, there_ref)
    bias = jnp.concatenate(
        [bias_of(ref, place_ref[1], samples, tokens) for ref in packs], axis=1
    )
    keys = jnp.concatenate([ref[:tokens, :] for ref in packs], axis=0)
    values = jnp.concatenate([ref[tokens : 2 * tokens, :] for ref in packs], axis=0)
    values = jnp.concatenate([values, jnp.ones((2 * tokens, HD), BF16)], axis=1)
    for first in range(0, samples, TILE):
        here = slice(first, first + TILE)
        rows = slice(first * ITEM, (first + TILE) * ITEM)
        q = q_ref[here].reshape(TILE * ITEM, HD)
        scores = dot_t(q, keys) * SCALE
        scores = scores.reshape(TILE, ITEM, 2 * tokens) + bias[here][:, None, :]
        scores = scores.reshape(TILE * ITEM, 2 * tokens)
        top = jnp.max(scores, axis=1, keepdims=True)
        weights = jnp.exp2(scores - top).astype(BF16)
        total = dot(weights, values)
        mass = total[:, HD:]
        total_ref[rows, :] = total[:, :HD] / mass
        log_ref[rows, :] = top + jnp.log2(mass)
    mine = pl.ds(pl.multiple_of(place_ref[0] * ITEM, ITEM), ITEM)
    log = log_ref[mine, :]
    own_log = own_log_ref[...]
    best = jnp.maximum(log, own_log)
    factor = jnp.exp2(log - best)
    own_factor = jnp.exp2(own_log - best)
    mass = factor + own_factor
    total_ref[mine, :] = (total_ref[mine, :] * factor + own_ref[...] * own_factor) / mass
    log_ref[mine, :] = best + jnp.log2(mass)
    shape = (ITEM, HD)
    pick = iota(shape, 0) == iota(shape, 1) % ITEM
    row = iota((STAT, HD), 0)
    inner = samples // 8
    for outer in range(samples // (HALVES * inner)):
        for half in range(HALVES):
            for last in range(inner):
                target = (outer * HALVES + half) * inner + last
                slices = []
                for turn in range(HALVES):
                    start = ((outer * HALVES + turn) * inner + last) * ITEM + half * PART
                    slices.append(slice(start, start + PART))
                part = jnp.concatenate([total_ref[rows, :] for rows in slices], axis=0)
                out_ref[target, :ITEM, :] = part.astype(BF16)
                log = jnp.concatenate([log_ref[rows, :] for rows in slices], axis=0)
                log = jnp.sum(jnp.where(pick, log, 0.0), axis=0, keepdims=True)
                high = log.astype(BF16).astype(F32)
                rest = log - high
                middle = rest.astype(BF16).astype(F32)
                low = rest - middle
                stat = jnp.where(row == 1, middle, jnp.where(row == 2, low, 0.0))
                stat = jnp.where(row == 0, high, stat)
                out_ref[target, ITEM:, :] = stat.astype(BF16)


def combine_kernel(part_ref, out_ref):
    shards = part_ref.shape[0]
    log_mass = jnp.sum(part_ref[:, ITEM:, :].astype(F32), axis=1)
    weights = jnp.exp2(log_mass - jnp.max(log_mass, axis=0, keepdims=True))
    weights = weights / jnp.sum(weights, axis=0, keepdims=True)
    per_lane = HD // ITEM
    groups = shards // per_lane
    lane = iota((groups, HD), 1) // ITEM
    packed = jnp.zeros((groups, HD), F32)
    for turn in range(per_lane):
        packed = jnp.where(lane == turn, weights[turn * groups : (turn + 1) * groups], packed)
    pick = iota((ITEM, HD), 0) == iota((ITEM, HD), 1) % ITEM
    factors = []
    rows = []
    for group in range(groups):
        factors.append(jnp.where(pick, packed[group : group + 1], 0.0))
        for turn in range(per_lane):
            rows.append(part_ref[group + turn * groups, :ITEM, :])
    factor = jnp.concatenate(factors, axis=1)
    high = factor.astype(BF16)
    low = (factor - high.astype(F32)).astype(BF16)
    total = dot(jnp.concatenate([high, low], axis=0), jnp.concatenate(rows, axis=0))
    attended = (total[:ITEM] + total[ITEM:]).astype(BF16)
    out_ref[...] = jnp.broadcast_to(attended[None], out_ref.shape)


def project_kernel(place_ref, x_ref, w_ref, other_ref, out_ref, rows_ref):
    peers = x_ref.shape[0]
    depth = HALF * HD
    rows_ref[...] = x_ref[...].reshape(peers * ITEM, HD).astype(F32)
    columns = []
    for head in range(HALF):
        pieces = [
            rows_ref[pl.ds(turn * PART + step * HALF + head, peers, stride=ITEM), :]
            for turn in range(HALVES)
            for step in range(STEPS)
        ]
        columns.append(jnp.concatenate(pieces, axis=0).astype(BF16))
    left = jnp.concatenate(columns, axis=1)
    half = place_ref[2]
    mine = pl.ds(pl.multiple_of(half * depth, depth), depth)
    parts = out_ref.shape[0] // HALVES
    outer = parts // HALVES
    for owner, weight in ((half, w_ref[mine, :]), (1 - half, other_ref[...])):
        product = dot(left, weight)
        for part in range(parts):
            first, turn = part // HALVES, part % HALVES
            size = peers // outer
            pieces = []
            for step in range(STEPS):
                start = (turn * STEPS + step) * peers + first * size
                pieces.append(product[start : start + size])
            out_ref[owner * parts + part] = jnp.concatenate(pieces, axis=0).astype(BF16)


def sum_kernel(x_ref, out_ref):
    total = jnp.sum(x_ref[...].astype(F32), axis=0)
    out_ref[...] = total.reshape(out_ref.shape).astype(BF16)


def call(kernel, name, out_shape, in_specs, out_specs, scratch=(), flops=0, moved=0):
    return pl.pallas_call(
        kernel,
        name=name,
        out_shape=out_shape,
        in_specs=in_specs,
        out_specs=out_specs,
        scratch_shapes=scratch,
        compiler_params=PARAMS,
        cost_estimate=pl.CostEstimate(flops=flops, bytes_accessed=moved, transcendentals=0),
    )


def swap(array, axes):
    return lax.all_to_all(array, axes, split_axis=0, concat_axis=0, tiled=True)


def shards(
    queries,
    prompt_keys,
    prompt_values,
    selected,
    cache_keys,
    cache_values,
    new_keys,
    new_values,
    positions,
    out_weight,
):
    struct = jax.ShapeDtypeStruct
    samples = lax.axis_size(SAMPLES)
    heads = lax.axis_size("head")
    tokens = prompt_keys.shape[0]
    depth, columns = HALF * HD, out_weight.shape[1]
    half = lax.axis_index("zl")
    place = jnp.stack([lax.axis_index(SAMPLES), lax.axis_index("yl"), half]).astype(jnp.int32)
    rows_scratch = pltpu.VMEM((ITEM, HD), F32)
    q = queries.reshape(STEPS, PER * HD)
    pair = [(0, 1), (1, 0)]

    spread = call(
        spread_kernel, "spread", struct((samples, ITEM, HD), BF16), [VMEM], VMEM, [rows_scratch]
    )(q)
    here = call(
        pack_kernel, "pack", struct((2 * tokens + FLAG, HD), BF16), [VMEM] * 3, VMEM
    )(prompt_keys, prompt_values, selected[:, 0, :].T)
    gathered = swap(spread, SAMPLES)
    there = lax.ppermute(here, "yl", pair)
    other_weight = lax.ppermute(
        lax.dynamic_slice_in_dim(out_weight, (1 - half) * depth, depth, axis=0), "zl", pair
    )
    own, own_log = call(
        own_kernel,
        "own",
        (struct((ITEM, HD), F32), struct((ITEM, HD), F32)),
        [VMEM] * 5 + [SMEM],
        (VMEM, VMEM),
        [rows_scratch],
        flops=10**6,
        moved=3 * 10**5,
    )(q, cache_keys[0], cache_values[0], new_keys[:, 0], new_values[:, 0], positions)
    partial = call(
        prompt_kernel,
        "prompt",
        struct((samples, ITEM + STAT, HD), BF16),
        [SMEM] + [VMEM] * 5,
        VMEM,
        [pltpu.VMEM((samples * ITEM, HD), F32)] * 2,
    )(place, gathered, here, there, own, own_log)
    received = swap(partial, SAMPLES)
    attended = call(
        combine_kernel, "combine", struct((samples, ITEM, HD), BF16), [VMEM], VMEM
    )(received)
    every = swap(attended, ("zh", "yh", "yl"))
    product = call(
        project_kernel,
        "project",
        struct((HALVES * heads, STEPS * 2 * samples // heads, columns), BF16),
        [SMEM] + [VMEM] * 3,
        VMEM,
        [pltpu.VMEM((samples * ITEM, HD), F32)],
    )(place, every, out_weight, other_weight)
    terms = swap(product, ("zl", "head"))
    return call(
        sum_kernel, "sum", struct((STEPS, 2 * samples // heads, columns), BF16), [VMEM], VMEM
    )(terms)


def solution(mesh):
    fine = Mesh(mesh.devices.reshape(4, 2, 4, 2, 8), ("zh", "zl", "yh", "yl", "head"))
    ctx = ("zh", "zl", "yh", "yl")
    placed = (
        P(None, ctx, "head"),
        P(ctx, "head"),
        P(ctx, "head"),
        P(None, "head", ctx),
        P(ctx, None, "head"),
        P(ctx, None, "head"),
        P(None, ctx, "head"),
        P(None, ctx, "head"),
        P(ctx),
        P("head", ctx),
    )
    return jax.shard_map(
        shards, mesh=fine, in_specs=placed, out_specs=P(None, "head", ctx), check_vma=False
    )
```

```python
import math

import jax
import jax.numpy as jnp
from jax import lax
from jax.experimental import pallas as pl
from jax.experimental.pallas import tpu as pltpu
from jax.sharding import Mesh
from jax.sharding import PartitionSpec as P

HD = 128
PER = 16
BLOCK = 64
STEPS = 2
ITEM = STEPS * PER
STAT = 8
FLAG = 16
NEGATIVE = -1e30
SCALE = math.log2(math.e) / math.sqrt(HD)
TILE = 4
CTX = ("zh", "zl", "yh", "yl")
FAR = ("zh", "yh")
NEAR = ("zl", "yl")

VMEM = pl.BlockSpec(memory_space=pltpu.VMEM)
SMEM = pl.BlockSpec(memory_space=pltpu.SMEM)
PARAMS = pltpu.CompilerParams(vmem_limit_bytes=24 * 1024 * 1024)
F32 = jnp.float32
BF16 = jnp.bfloat16


def dot(a, b):
    return lax.dot_general(a, b, (((1,), (0,)), ((), ())), preferred_element_type=F32)


def dot_t(a, b):
    return lax.dot_general(a, b, (((1,), (1,)), ((), ())), preferred_element_type=F32)


def iota(shape, dim):
    return lax.broadcasted_iota(jnp.int32, shape, dim)


def item_rows(q_ref, rows_ref):
    whole = q_ref[...].astype(F32)
    for step in range(STEPS):
        for head in range(PER):
            row = step * PER + head
            rows_ref[row : row + 1, :] = whole[step : step + 1, head * HD : (head + 1) * HD]
    return rows_ref[...]


def to_lanes(column, count):
    shape = (count, ITEM, HD)
    pick = iota(shape, 1) == iota(shape, 2) % ITEM
    return jnp.sum(jnp.where(pick, column.reshape(shape), 0.0), axis=1)


def spread_kernel(q_ref, out_ref, rows_ref):
    rows = item_rows(q_ref, rows_ref).astype(BF16)
    out_ref[...] = jnp.broadcast_to(rows[None], out_ref.shape)


def pack_kernel(k_ref, v_ref, sel_ref, out_ref):
    tokens = k_ref.shape[0]
    out_ref[:tokens, :] = k_ref[...]
    out_ref[tokens : 2 * tokens, :] = v_ref[...]
    slots, samples = sel_ref.shape
    number = iota((FLAG, samples), 0)
    bias = jnp.full((FLAG, samples), NEGATIVE, F32)
    for slot in range(slots):
        bias = jnp.where(sel_ref[slot : slot + 1, :] == number, 0.0, bias)
    bias = jnp.concatenate([bias, jnp.zeros((FLAG, HD - samples), F32)], axis=1)
    out_ref[2 * tokens :, :] = bias.astype(BF16)


def own_kernel(q_ref, ck_ref, cv_ref, nk_ref, nv_ref, pos_ref, out_ref, log_ref, rows_ref):
    rows = item_rows(q_ref, rows_ref)
    slots = ck_ref.shape[0]
    scores = dot_t(rows.astype(BF16), ck_ref[...]) * SCALE
    alive = iota((ITEM, slots), 1) < pos_ref[0]
    scores = jnp.where(alive, scores, NEGATIVE)
    top = jnp.max(scores, axis=1, keepdims=True)
    step = iota((ITEM, 1), 0) // PER
    new_scores = []
    for token in range(STEPS):
        key = nk_ref[token : token + 1, :].astype(F32)
        score = jnp.sum(rows * key, axis=1, keepdims=True) * SCALE
        score = jnp.where(step >= token, score, NEGATIVE)
        new_scores.append(score)
        top = jnp.maximum(top, score)
    weights = jnp.where(alive, jnp.exp2(scores - top), 0.0)
    mass = jnp.sum(weights, axis=1, keepdims=True)
    total = dot(weights.astype(BF16), cv_ref[...])
    for token in range(STEPS):
        weight = jnp.where(step >= token, jnp.exp2(new_scores[token] - top), 0.0)
        mass = mass + weight
        value = nv_ref[token : token + 1, :].astype(F32)
        total = total + weight.astype(BF16).astype(F32) * value
    out_ref[...] = total / mass
    log_mass = jnp.broadcast_to(top + jnp.log2(mass), (ITEM, HD))
    log_ref[...] = jnp.broadcast_to(to_lanes(log_mass, 1), log_ref.shape)


def prompt_kernel(place_ref, q_ref, *refs):
    *pack_refs, out_ref, keys_ref = refs
    samples = q_ref.shape[0]
    tokens = (pack_refs[0].shape[0] - FLAG) // 2
    widen = iota((tokens, FLAG), 0) // BLOCK == iota((tokens, FLAG), 1)
    widen = widen.astype(F32).astype(BF16)
    for index, ref in enumerate(pack_refs):
        keys_ref[index, :, :HD] = ref[:tokens, :]
        keys_ref[index, :, HD:] = dot(widen, ref[2 * tokens :, :]).astype(BF16)
    ones = jnp.ones((tokens, HD), BF16)
    count = TILE * ITEM
    number = iota((count, HD), 0) // ITEM
    for first in range(0, samples, TILE):
        here = slice(first, first + TILE)
        q = q_ref[here].reshape(count, HD)
        sample = (first + number) // 4 * 16 + (first + number) % 4 * 2 + place_ref[0]
        mine = (iota((count, HD), 1) == sample).astype(F32).astype(BF16)
        q = jnp.concatenate([q, mine], axis=1)
        scores = [dot_t(q, keys_ref[index]) for index in range(len(pack_refs))]
        top = scores[0]
        for score in scores[1:]:
            top = jnp.maximum(top, score)
        top = jnp.max(top, axis=1, keepdims=True)
        total = jnp.zeros((count, 2 * HD), F32)
        for score, ref in zip(scores, pack_refs):
            weights = jnp.exp2((score - top) * SCALE).astype(BF16)
            values = jnp.concatenate([ref[tokens : 2 * tokens, :], ones], axis=1)
            total = total + dot(weights, values)
        mass = total[:, HD:]
        out_ref[here, :ITEM, :] = (total[:, :HD] / mass).astype(BF16).reshape(TILE, ITEM, HD)
        log_mass = to_lanes(top * SCALE + jnp.log2(mass), TILE)
        high = log_mass.astype(BF16).astype(F32)
        rest = log_mass - high
        middle = rest.astype(BF16).astype(F32)
        low = rest - middle
        shape = (TILE, STAT, HD)
        row = iota(shape, 1)
        stat = jnp.where(row == 0, jnp.broadcast_to(high[:, None, :], shape), 0.0)
        stat = jnp.where(row == 1, jnp.broadcast_to(middle[:, None, :], shape), stat)
        stat = jnp.where(row == 2, jnp.broadcast_to(low[:, None, :], shape), stat)
        out_ref[here, ITEM:, :] = stat.astype(BF16)


def combine_kernel(part_ref, own_ref, own_log_ref, out_ref):
    shards = part_ref.shape[0]
    log_mass = jnp.sum(part_ref[:, ITEM:, :].astype(F32), axis=1)
    own_log = own_log_ref[0:1, :]
    best = jnp.maximum(jnp.max(log_mass, axis=0, keepdims=True), own_log)
    weights = jnp.exp2(log_mass - best)
    own_weight = jnp.exp2(own_log - best)
    whole = jnp.sum(weights, axis=0, keepdims=True) + own_weight
    weights = weights / whole
    own_weight = own_weight / whole
    per_lane = HD // ITEM
    groups = shards // per_lane
    lane = iota((groups, HD), 1) // ITEM
    packed = jnp.zeros((groups, HD), F32)
    for turn in range(per_lane):
        packed = jnp.where(lane == turn, weights[turn * groups : (turn + 1) * groups], packed)
    pick = iota((ITEM, HD), 0) == iota((ITEM, HD), 1) % ITEM
    factors = []
    rows = []
    for group in range(groups):
        factors.append(jnp.where(pick, packed[group : group + 1], 0.0))
        for turn in range(per_lane):
            rows.append(part_ref[group + turn * groups, :ITEM, :])
    factor = jnp.concatenate(factors, axis=1)
    high = factor.astype(BF16)
    low = (factor - high.astype(F32)).astype(BF16)
    total = dot(jnp.concatenate([high, low], axis=0), jnp.concatenate(rows, axis=0))
    total = total[:ITEM] + total[ITEM:]
    own_column = jnp.sum(
        jnp.where(iota((ITEM, HD), 0) == iota((ITEM, HD), 1), own_weight, 0.0),
        axis=1,
        keepdims=True,
    )
    attended = (total + own_column * own_ref[...]).astype(BF16)
    out_ref[...] = jnp.broadcast_to(attended[None], out_ref.shape)


def project_kernel(x_ref, w_ref, out_ref, rows_ref):
    samples = x_ref.shape[0]
    parts = out_ref.shape[0]
    per_part = samples // parts
    rows_ref[...] = x_ref[...].reshape(samples * ITEM, HD).astype(F32)
    columns = []
    for head in range(PER):
        pieces = [
            rows_ref[pl.ds(step * PER + head, samples, stride=ITEM), :] for step in range(STEPS)
        ]
        columns.append(jnp.concatenate(pieces, axis=0).astype(BF16))
    product = dot(jnp.concatenate(columns, axis=1), w_ref[...])
    for part in range(parts):
        pieces = [
            product[step * samples + part * per_part : step * samples + (part + 1) * per_part]
            for step in range(STEPS)
        ]
        out_ref[part] = jnp.concatenate(pieces, axis=0).astype(out_ref.dtype)


def sum_kernel(x_ref, out_ref):
    total = jnp.sum(x_ref[...].astype(F32), axis=0)
    out_ref[...] = total.reshape(out_ref.shape).astype(BF16)


def call(kernel, name, out_shape, in_specs, out_specs, scratch=(), flops=0, moved=0):
    return pl.pallas_call(
        kernel,
        name=name,
        out_shape=out_shape,
        in_specs=in_specs,
        out_specs=out_specs,
        scratch_shapes=scratch,
        compiler_params=PARAMS,
        cost_estimate=pl.CostEstimate(flops=flops, bytes_accessed=moved, transcendentals=0),
    )


def swap(array, axes):
    return lax.all_to_all(array, axes, split_axis=0, concat_axis=0, tiled=True)


def shards(
    queries,
    prompt_keys,
    prompt_values,
    selected,
    cache_keys,
    cache_values,
    new_keys,
    new_values,
    positions,
    out_weight,
):
    struct = jax.ShapeDtypeStruct
    samples = lax.axis_size(CTX)
    far = lax.axis_size(FAR)
    heads = lax.axis_size("head")
    tokens = prompt_keys.shape[0]
    columns = out_weight.shape[1]
    place = (8 * lax.axis_index("zl") + lax.axis_index("yl")).astype(jnp.int32).reshape(1)
    rows_scratch = pltpu.VMEM((ITEM, HD), F32)
    q = queries.reshape(STEPS, PER * HD)

    spread = call(
        spread_kernel, "spread", struct((far, ITEM, HD), BF16), [VMEM], VMEM, [rows_scratch]
    )(q)
    here = call(
        pack_kernel, "pack", struct((2 * tokens + FLAG, HD), BF16), [VMEM] * 3, VMEM
    )(prompt_keys, prompt_values, selected[:, 0, :].T)
    gathered = swap(spread, FAR)
    packs = [
        here,
        lax.ppermute(here, "yl", [(0, 1), (1, 0)]),
        lax.ppermute(here, "zl", [(0, 1), (1, 0)]),
        lax.ppermute(here, NEAR, [(0, 3), (1, 2), (2, 1), (3, 0)]),
    ]
    own, own_log = call(
        own_kernel,
        "own",
        (struct((ITEM, HD), F32), struct((8, HD), F32)),
        [VMEM] * 5 + [SMEM],
        (VMEM, VMEM),
        [rows_scratch],
        flops=10**6,
        moved=3 * 10**5,
    )(q, cache_keys[0], cache_values[0], new_keys[:, 0], new_values[:, 0], positions)
    partial = call(
        prompt_kernel,
        "prompt",
        struct((far, ITEM + STAT, HD), BF16),
        [SMEM] + [VMEM] * 5,
        VMEM,
        [pltpu.VMEM((4, tokens, 2 * HD), BF16)],
    )(place, gathered, *packs)
    received = swap(partial, FAR)
    attended = call(
        combine_kernel, "combine", struct((samples, ITEM, HD), BF16), [VMEM] * 3, VMEM
    )(received, own, own_log)
    every = swap(attended, CTX)
    product = call(
        project_kernel,
        "project",
        struct((heads, STEPS * samples // heads, columns), F32),
        [VMEM] * 2,
        VMEM,
        [pltpu.VMEM((samples * ITEM, HD), F32)],
    )(every, out_weight)
    terms = swap(product, "head")
    return call(
        sum_kernel, "sum", struct((STEPS, samples // heads, columns), BF16), [VMEM], VMEM
    )(terms)


def solution(mesh):
    fine = Mesh(mesh.devices.reshape(4, 2, 4, 2, 8), (*CTX, "head"))
    placed = (
        P(None, CTX, "head"),
        P(CTX, "head"),
        P(CTX, "head"),
        P(None, "head", CTX),
        P(CTX, None, "head"),
        P(CTX, None, "head"),
        P(None, CTX, "head"),
        P(None, CTX, "head"),
        P(CTX),
        P("head", CTX),
    )
    return jax.shard_map(
        shards, mesh=fine, in_specs=placed, out_specs=P(None, "head", CTX), check_vma=False
    )
```

```python
import math

import jax
import jax.numpy as jnp
from jax import lax
from jax.experimental import pallas as pl
from jax.experimental.pallas import tpu as pltpu
from jax.sharding import Mesh
from jax.sharding import PartitionSpec as P

HD = 128
PER = 16
BLOCK = 64
STEPS = 2
ITEM = STEPS * PER
STAT = 8
FLAG = 16
NEGATIVE = -1e30
SCALE = math.log2(math.e) / math.sqrt(HD)
TILE = 4
CTX = ("z", "yh", "yl")
FAR = ("z", "yh")
NEAR = "yl"

VMEM = pl.BlockSpec(memory_space=pltpu.VMEM)
SMEM = pl.BlockSpec(memory_space=pltpu.SMEM)
PARAMS = pltpu.CompilerParams(vmem_limit_bytes=24 * 1024 * 1024)
F32 = jnp.float32
BF16 = jnp.bfloat16


def dot(a, b):
    return lax.dot_general(a, b, (((1,), (0,)), ((), ())), preferred_element_type=F32)


def dot_t(a, b):
    return lax.dot_general(a, b, (((1,), (1,)), ((), ())), preferred_element_type=F32)


def iota(shape, dim):
    return lax.broadcasted_iota(jnp.int32, shape, dim)


def item_rows(q_ref, rows_ref):
    whole = q_ref[...].astype(F32)
    for step in range(STEPS):
        for head in range(PER):
            row = step * PER + head
            rows_ref[row : row + 1, :] = whole[step : step + 1, head * HD : (head + 1) * HD]
    return rows_ref[...]


def to_lanes(column, count):
    shape = (count, ITEM, HD)
    pick = iota(shape, 1) == iota(shape, 2) % ITEM
    return jnp.sum(jnp.where(pick, column.reshape(shape), 0.0), axis=1)


def spread_kernel(q_ref, out_ref, rows_ref):
    rows = item_rows(q_ref, rows_ref).astype(BF16)
    out_ref[...] = jnp.broadcast_to(rows[None], out_ref.shape)


def pack_kernel(k_ref, v_ref, sel_ref, out_ref):
    tokens = k_ref.shape[0]
    out_ref[:tokens, :] = k_ref[...]
    out_ref[tokens : 2 * tokens, :] = v_ref[...]
    slots, samples = sel_ref.shape
    number = iota((FLAG, samples), 0)
    bias = jnp.full((FLAG, samples), NEGATIVE, F32)
    for slot in range(slots):
        bias = jnp.where(sel_ref[slot : slot + 1, :] == number, 0.0, bias)
    bias = jnp.concatenate([bias, jnp.zeros((FLAG, HD - samples), F32)], axis=1)
    out_ref[2 * tokens :, :] = bias.astype(BF16)


def own_kernel(q_ref, ck_ref, cv_ref, nk_ref, nv_ref, pos_ref, out_ref, log_ref, rows_ref):
    rows = item_rows(q_ref, rows_ref)
    slots = ck_ref.shape[0]
    scores = dot_t(rows.astype(BF16), ck_ref[...]) * SCALE
    alive = iota((ITEM, slots), 1) < pos_ref[0]
    scores = jnp.where(alive, scores, NEGATIVE)
    top = jnp.max(scores, axis=1, keepdims=True)
    step = iota((ITEM, 1), 0) // PER
    new_scores = []
    for token in range(STEPS):
        key = nk_ref[token : token + 1, :].astype(F32)
        score = jnp.sum(rows * key, axis=1, keepdims=True) * SCALE
        score = jnp.where(step >= token, score, NEGATIVE)
        new_scores.append(score)
        top = jnp.maximum(top, score)
    weights = jnp.where(alive, jnp.exp2(scores - top), 0.0)
    mass = jnp.sum(weights, axis=1, keepdims=True)
    total = dot(weights.astype(BF16), cv_ref[...])
    for token in range(STEPS):
        weight = jnp.where(step >= token, jnp.exp2(new_scores[token] - top), 0.0)
        mass = mass + weight
        value = nv_ref[token : token + 1, :].astype(F32)
        total = total + weight.astype(BF16).astype(F32) * value
    out_ref[...] = total / mass
    log_mass = jnp.broadcast_to(top + jnp.log2(mass), (ITEM, HD))
    log_ref[...] = jnp.broadcast_to(to_lanes(log_mass, 1), log_ref.shape)


def prompt_kernel(place_ref, q_ref, *refs):
    *pack_refs, out_ref, keys_ref = refs
    samples = q_ref.shape[0]
    tokens = (pack_refs[0].shape[0] - FLAG) // 2
    widen = iota((FLAG, tokens), 1) // BLOCK == iota((FLAG, tokens), 0)
    widen = widen.astype(F32).astype(BF16)
    for index, ref in enumerate(pack_refs):
        place = slice(index * tokens, (index + 1) * tokens)
        keys_ref[:HD, place] = ref[:tokens, :].T
        bias = lax.dot_general(
            ref[2 * tokens :, :], widen, (((0,), (0,)), ((), ())), preferred_element_type=F32
        )
        keys_ref[HD:, place] = bias.astype(BF16)
    ones = jnp.ones((tokens, HD), BF16)
    count = TILE * ITEM
    number = iota((count, HD), 0) // ITEM
    for first in range(0, samples, TILE):
        here = slice(first, first + TILE)
        q = q_ref[here].reshape(count, HD)
        mine = iota((count, HD), 1) == 2 * (first + number) + place_ref[0]
        q = jnp.concatenate([q, mine.astype(F32).astype(BF16)], axis=1)
        scores = []
        for index in range(len(pack_refs)):
            scores.append(dot(q, keys_ref[:, index * tokens : (index + 1) * tokens]))
        top = scores[0]
        for score in scores[1:]:
            top = jnp.maximum(top, score)
        top = jnp.max(top, axis=1, keepdims=True)
        total = jnp.zeros((count, 2 * HD), F32)
        for score, ref in zip(scores, pack_refs):
            weights = jnp.exp2((score - top) * SCALE).astype(BF16)
            values = jnp.concatenate([ref[tokens : 2 * tokens, :], ones], axis=1)
            total = total + dot(weights, values)
        mass = total[:, HD:]
        out_ref[here, :ITEM, :] = (total[:, :HD] / mass).astype(BF16).reshape(TILE, ITEM, HD)
        log_mass = to_lanes(top * SCALE + jnp.log2(mass), TILE)
        high = log_mass.astype(BF16).astype(F32)
        rest = log_mass - high
        middle = rest.astype(BF16).astype(F32)
        low = rest - middle
        shape = (TILE, STAT, HD)
        row = iota(shape, 1)
        stat = jnp.where(row == 0, jnp.broadcast_to(high[:, None, :], shape), 0.0)
        stat = jnp.where(row == 1, jnp.broadcast_to(middle[:, None, :], shape), stat)
        stat = jnp.where(row == 2, jnp.broadcast_to(low[:, None, :], shape), stat)
        out_ref[here, ITEM:, :] = stat.astype(BF16)


def combine_kernel(part_ref, own_ref, own_log_ref, out_ref):
    shards = part_ref.shape[0]
    log_mass = jnp.sum(part_ref[:, ITEM:, :].astype(F32), axis=1)
    own_log = own_log_ref[0:1, :]
    best = jnp.maximum(jnp.max(log_mass, axis=0, keepdims=True), own_log)
    weights = jnp.exp2(log_mass - best)
    own_weight = jnp.exp2(own_log - best)
    whole = jnp.sum(weights, axis=0, keepdims=True) + own_weight
    weights = weights / whole
    own_weight = own_weight / whole
    per_lane = HD // ITEM
    groups = shards // per_lane
    lane = iota((groups, HD), 1) // ITEM
    packed = jnp.zeros((groups, HD), F32)
    for turn in range(per_lane):
        packed = jnp.where(lane == turn, weights[turn * groups : (turn + 1) * groups], packed)
    pick = iota((ITEM, HD), 0) == iota((ITEM, HD), 1) % ITEM
    factors = []
    rows = []
    for group in range(groups):
        factors.append(jnp.where(pick, packed[group : group + 1], 0.0))
        for turn in range(per_lane):
            rows.append(part_ref[group + turn * groups, :ITEM, :])
    factor = jnp.concatenate(factors, axis=1)
    high = factor.astype(BF16)
    low = (factor - high.astype(F32)).astype(BF16)
    total = dot(jnp.concatenate([high, low], axis=0), jnp.concatenate(rows, axis=0))
    total = total[:ITEM] + total[ITEM:]
    own_column = jnp.sum(
        jnp.where(iota((ITEM, HD), 0) == iota((ITEM, HD), 1), own_weight, 0.0),
        axis=1,
        keepdims=True,
    )
    attended = (total + own_column * own_ref[...]).astype(BF16)
    out_ref[...] = jnp.broadcast_to(attended[None], out_ref.shape)


def project_kernel(x_ref, w_ref, out_ref, rows_ref):
    samples = x_ref.shape[0]
    parts = out_ref.shape[0]
    per_part = samples // parts
    rows_ref[...] = x_ref[...].reshape(samples * ITEM, HD).astype(F32)
    columns = []
    for head in range(PER):
        pieces = [
            rows_ref[pl.ds(step * PER + head, samples, stride=ITEM), :] for step in range(STEPS)
        ]
        columns.append(jnp.concatenate(pieces, axis=0).astype(BF16))
    product = dot(jnp.concatenate(columns, axis=1), w_ref[...])
    for part in range(parts):
        pieces = [
            product[step * samples + part * per_part : step * samples + (part + 1) * per_part]
            for step in range(STEPS)
        ]
        out_ref[part] = jnp.concatenate(pieces, axis=0).astype(out_ref.dtype)


def sum_kernel(x_ref, out_ref):
    total = jnp.sum(x_ref[...].astype(F32), axis=0)
    out_ref[...] = total.reshape(out_ref.shape).astype(BF16)


def call(kernel, name, out_shape, in_specs, out_specs, scratch=(), flops=0, moved=0):
    return pl.pallas_call(
        kernel,
        name=name,
        out_shape=out_shape,
        in_specs=in_specs,
        out_specs=out_specs,
        scratch_shapes=scratch,
        compiler_params=PARAMS,
        cost_estimate=pl.CostEstimate(flops=flops, bytes_accessed=moved, transcendentals=0),
    )


def swap(array, axes):
    return lax.all_to_all(array, axes, split_axis=0, concat_axis=0, tiled=True)


def shards(
    queries,
    prompt_keys,
    prompt_values,
    selected,
    cache_keys,
    cache_values,
    new_keys,
    new_values,
    positions,
    out_weight,
):
    struct = jax.ShapeDtypeStruct
    samples = lax.axis_size(CTX)
    far = lax.axis_size(FAR)
    heads = lax.axis_size("head")
    tokens = prompt_keys.shape[0]
    columns = out_weight.shape[1]
    place = lax.axis_index(NEAR).astype(jnp.int32).reshape(1)
    rows_scratch = pltpu.VMEM((ITEM, HD), F32)
    q = queries.reshape(STEPS, PER * HD)

    spread = call(
        spread_kernel, "spread", struct((far, ITEM, HD), BF16), [VMEM], VMEM, [rows_scratch]
    )(q)
    here = call(
        pack_kernel, "pack", struct((2 * tokens + FLAG, HD), BF16), [VMEM] * 3, VMEM
    )(prompt_keys, prompt_values, selected[:, 0, :].T)
    gathered = swap(spread, FAR)
    there = lax.ppermute(here, NEAR, [(0, 1), (1, 0)])
    own, own_log = call(
        own_kernel,
        "own",
        (struct((ITEM, HD), F32), struct((8, HD), F32)),
        [VMEM] * 5 + [SMEM],
        (VMEM, VMEM),
        [rows_scratch],
        flops=10**6,
        moved=3 * 10**5,
    )(q, cache_keys[0], cache_values[0], new_keys[:, 0], new_values[:, 0], positions)
    partial = call(
        prompt_kernel,
        "prompt",
        struct((far, ITEM + STAT, HD), BF16),
        [SMEM] + [VMEM] * 3,
        VMEM,
        [pltpu.VMEM((2 * HD, 2 * tokens), BF16)],
    )(place, gathered, here, there)
    received = swap(partial, FAR)
    attended = call(
        combine_kernel, "combine", struct((samples, ITEM, HD), BF16), [VMEM] * 3, VMEM
    )(received, own, own_log)
    every = swap(attended, CTX)
    product = call(
        project_kernel,
        "project",
        struct((heads, STEPS * samples // heads, columns), F32),
        [VMEM] * 2,
        VMEM,
        [pltpu.VMEM((samples * ITEM, HD), F32)],
    )(every, out_weight)
    terms = swap(product, "head")
    return call(
        sum_kernel, "sum", struct((STEPS, samples // heads, columns), BF16), [VMEM], VMEM
    )(terms)


def solution(mesh):
    fine = Mesh(mesh.devices.reshape(8, 4, 2, 8), (*CTX, "head"))
    placed = (
        P(None, CTX, "head"),
        P(CTX, "head"),
        P(CTX, "head"),
        P(None, "head", CTX),
        P(CTX, None, "head"),
        P(CTX, None, "head"),
        P(None, CTX, "head"),
        P(None, CTX, "head"),
        P(CTX),
        P("head", CTX),
    )
    return jax.shard_map(
        shards, mesh=fine, in_specs=placed, out_specs=P(None, "head", CTX), check_vma=False
    )
```

```python
import math

import jax
import jax.numpy as jnp
from jax import lax
from jax.experimental import pallas as pl
from jax.experimental.pallas import tpu as pltpu
from jax.sharding import Mesh
from jax.sharding import PartitionSpec as P

HD = 128
PER = 16
BLOCK = 64
STEPS = 2
ITEM = STEPS * PER
STAT = 8
FLAG = 16
NEGATIVE = -1e30
SCALE = math.log2(math.e) / math.sqrt(HD)
TILE = 4
CTX = ("zh", "zl", "yh", "yl")
FAR = ("zh", "yh")
NEAR = ("zl", "yl")

VMEM = pl.BlockSpec(memory_space=pltpu.VMEM)
SMEM = pl.BlockSpec(memory_space=pltpu.SMEM)
ANY = pl.BlockSpec(memory_space=pl.ANY)
F32 = jnp.float32
BF16 = jnp.bfloat16


def dot(a, b):
    return lax.dot_general(a, b, (((1,), (0,)), ((), ())), preferred_element_type=F32)


def dot_t(a, b):
    return lax.dot_general(a, b, (((1,), (1,)), ((), ())), preferred_element_type=F32)


def iota(shape, dim):
    return lax.broadcasted_iota(jnp.int32, shape, dim)


def item_rows(q_ref, rows_ref):
    whole = q_ref[...].astype(F32)
    for step in range(STEPS):
        for head in range(PER):
            row = step * PER + head
            rows_ref[row : row + 1, :] = whole[step : step + 1, head * HD : (head + 1) * HD]
    return rows_ref[...]


def to_lanes(column, count):
    shape = (count, ITEM, HD)
    pick = iota(shape, 1) == iota(shape, 2) % ITEM
    return jnp.sum(jnp.where(pick, column.reshape(shape), 0.0), axis=1)


def spread_kernel(q_ref, out_ref, rows_ref):
    rows = item_rows(q_ref, rows_ref).astype(BF16)
    out_ref[...] = jnp.broadcast_to(rows[None], out_ref.shape)


def pack_kernel(k_hbm, v_hbm, sel_hbm, out_ref, sel_ref, sems):
    tokens = k_hbm.shape[0]
    copies = [
        pltpu.make_async_copy(sel_hbm, sel_ref, sems.at[0]),
        pltpu.make_async_copy(k_hbm, out_ref.at[:tokens], sems.at[1]),
        pltpu.make_async_copy(v_hbm, out_ref.at[tokens : 2 * tokens], sems.at[2]),
    ]
    for copy in copies:
        copy.start()
    copies[0].wait()
    slots, samples = sel_ref.shape
    number = iota((FLAG, samples), 0)
    bias = jnp.full((FLAG, samples), NEGATIVE, F32)
    for slot in range(slots):
        bias = jnp.where(sel_ref[slot : slot + 1, :] == number, 0.0, bias)
    bias = jnp.concatenate([bias, jnp.zeros((FLAG, HD - samples), F32)], axis=1)
    out_ref[2 * tokens :, :] = bias.astype(BF16)
    for copy in copies[1:]:
        copy.wait()


def own_kernel(q_ref, ck_ref, cv_ref, nk_ref, nv_ref, pos_ref, out_ref, log_ref, rows_ref):
    rows = item_rows(q_ref, rows_ref)
    slots = ck_ref.shape[0]
    scores = dot_t(rows.astype(BF16), ck_ref[...]) * SCALE
    alive = iota((ITEM, slots), 1) < pos_ref[0]
    scores = jnp.where(alive, scores, NEGATIVE)
    top = jnp.max(scores, axis=1, keepdims=True)
    step = iota((ITEM, 1), 0) // PER
    new_scores = []
    for token in range(STEPS):
        key = nk_ref[token : token + 1, :].astype(F32)
        score = jnp.sum(rows * key, axis=1, keepdims=True) * SCALE
        score = jnp.where(step >= token, score, NEGATIVE)
        new_scores.append(score)
        top = jnp.maximum(top, score)
    weights = jnp.where(alive, jnp.exp2(scores - top), 0.0)
    mass = jnp.sum(weights, axis=1, keepdims=True)
    total = dot(weights.astype(BF16), cv_ref[...])
    for token in range(STEPS):
        weight = jnp.where(step >= token, jnp.exp2(new_scores[token] - top), 0.0)
        mass = mass + weight
        value = nv_ref[token : token + 1, :].astype(F32)
        total = total + weight.astype(BF16).astype(F32) * value
    out_ref[...] = total / mass
    log_mass = jnp.broadcast_to(top + jnp.log2(mass), (ITEM, HD))
    log_ref[...] = jnp.broadcast_to(to_lanes(log_mass, 1), log_ref.shape)


def prompt_kernel(place_ref, own_ref, q_ref, *refs):
    *pack_refs, out_ref, keys_ref = refs
    samples = q_ref.shape[0]
    tokens = (pack_refs[0].shape[0] - FLAG) // 2
    widen = iota((FLAG, tokens), 1) // BLOCK == iota((FLAG, tokens), 0)
    widen = widen.astype(F32).astype(BF16)
    for index, ref in enumerate(pack_refs):
        place = slice(index * tokens, (index + 1) * tokens)
        keys_ref[:HD, place] = ref[:tokens, :].T
        bias = lax.dot_general(
            ref[2 * tokens :, :], widen, (((0,), (0,)), ((), ())), preferred_element_type=F32
        )
        keys_ref[HD:, place] = bias.astype(BF16)
    ones = jnp.ones((tokens, HD), BF16)
    count = TILE * ITEM
    number = iota((count, HD), 0) // ITEM
    for first in range(0, samples, TILE):
        here = slice(first, first + TILE)
        q = q_ref[here].reshape(count, HD)
        sample = (first + number) // 4 * 16 + (first + number) % 4 * 2 + place_ref[0]
        mine = iota((count, HD), 1) == sample
        q = jnp.concatenate([q, mine.astype(F32).astype(BF16)], axis=1)
        scores = []
        for index in range(len(pack_refs)):
            scores.append(dot(q, keys_ref[:, index * tokens : (index + 1) * tokens]))
        top = scores[0]
        for score in scores[1:]:
            top = jnp.maximum(top, score)
        top = jnp.max(top, axis=1, keepdims=True)
        total = jnp.zeros((count, 2 * HD), F32)
        for score, ref in zip(scores, pack_refs):
            weights = jnp.exp2((score - top) * SCALE).astype(BF16)
            values = jnp.concatenate([ref[tokens : 2 * tokens, :], ones], axis=1)
            total = total + dot(weights, values)
        mass = total[:, HD:]
        out_ref[here, :ITEM, :] = (total[:, :HD] / mass).astype(BF16).reshape(TILE, ITEM, HD)
        log_mass = to_lanes(top * SCALE + jnp.log2(mass), TILE)
        high = log_mass.astype(BF16).astype(F32)
        rest = log_mass - high
        middle = rest.astype(BF16).astype(F32)
        low = rest - middle
        shape = (TILE, STAT, HD)
        row = iota(shape, 1)
        stat = jnp.where(row == 0, jnp.broadcast_to(high[:, None, :], shape), 0.0)
        stat = jnp.where(row == 1, jnp.broadcast_to(middle[:, None, :], shape), stat)
        stat = jnp.where(row == 2, jnp.broadcast_to(low[:, None, :], shape), stat)
        out_ref[here, ITEM:, :] = stat.astype(BF16)


def combine_kernel(part_ref, own_ref, own_log_ref, out_ref):
    shards = part_ref.shape[0]
    log_mass = jnp.sum(part_ref[:, ITEM:, :].astype(F32), axis=1)
    own_log = own_log_ref[0:1, :]
    best = jnp.maximum(jnp.max(log_mass, axis=0, keepdims=True), own_log)
    weights = jnp.exp2(log_mass - best)
    own_weight = jnp.exp2(own_log - best)
    whole = jnp.sum(weights, axis=0, keepdims=True) + own_weight
    weights = weights / whole
    own_weight = own_weight / whole
    per_lane = HD // ITEM
    groups = shards // per_lane
    lane = iota((groups, HD), 1) // ITEM
    packed = jnp.zeros((groups, HD), F32)
    for turn in range(per_lane):
        packed = jnp.where(lane == turn, weights[turn * groups : (turn + 1) * groups], packed)
    pick = iota((ITEM, HD), 0) == iota((ITEM, HD), 1) % ITEM
    factors = []
    rows = []
    for group in range(groups):
        factors.append(jnp.where(pick, packed[group : group + 1], 0.0))
        for turn in range(per_lane):
            rows.append(part_ref[group + turn * groups, :ITEM, :])
    factor = jnp.concatenate(factors, axis=1)
    high = factor.astype(BF16)
    low = (factor - high.astype(F32)).astype(BF16)
    total = dot(jnp.concatenate([high, low], axis=0), jnp.concatenate(rows, axis=0))
    total = total[:ITEM] + total[ITEM:]
    own_column = jnp.sum(
        jnp.where(iota((ITEM, HD), 0) == iota((ITEM, HD), 1), own_weight, 0.0),
        axis=1,
        keepdims=True,
    )
    attended = (total + own_column * own_ref[...]).astype(BF16)
    out_ref[...] = jnp.broadcast_to(attended[None], out_ref.shape)


def project_kernel(x_ref, w_ref, out_ref, rows_ref):
    samples = x_ref.shape[0]
    parts = out_ref.shape[0]
    per_part = samples // parts
    rows_ref[...] = x_ref[...].reshape(samples * ITEM, HD).astype(F32)
    columns = []
    for head in range(PER):
        pieces = [
            rows_ref[pl.ds(step * PER + head, samples, stride=ITEM), :] for step in range(STEPS)
        ]
        columns.append(jnp.concatenate(pieces, axis=0).astype(BF16))
    product = dot(jnp.concatenate(columns, axis=1), w_ref[...])
    for part in range(parts):
        pieces = [
            product[step * samples + part * per_part : step * samples + (part + 1) * per_part]
            for step in range(STEPS)
        ]
        out_ref[part] = jnp.concatenate(pieces, axis=0).astype(out_ref.dtype)


def sum_kernel(x_ref, out_ref):
    total = jnp.sum(x_ref[...].astype(F32), axis=0)
    out_ref[...] = total.reshape(out_ref.shape).astype(BF16)


def call(
    kernel, name, out_shape, in_specs, out_specs, scratch=(), flops=0, moved=0, vmem=24
):
    return pl.pallas_call(
        kernel,
        name=name,
        out_shape=out_shape,
        in_specs=in_specs,
        out_specs=out_specs,
        scratch_shapes=scratch,
        compiler_params=pltpu.CompilerParams(vmem_limit_bytes=vmem * 1024 * 1024),
        cost_estimate=pl.CostEstimate(flops=flops, bytes_accessed=moved, transcendentals=0),
    )


def swap(array, axes):
    return lax.all_to_all(array, axes, split_axis=0, concat_axis=0, tiled=True)


def shards(
    queries,
    prompt_keys,
    prompt_values,
    selected,
    cache_keys,
    cache_values,
    new_keys,
    new_values,
    positions,
    out_weight,
):
    struct = jax.ShapeDtypeStruct
    samples = lax.axis_size(CTX)
    far = lax.axis_size(FAR)
    heads = lax.axis_size("head")
    tokens = prompt_keys.shape[0]
    columns = out_weight.shape[1]
    place = (8 * lax.axis_index("zl") + lax.axis_index("yl")).astype(jnp.int32).reshape(1)
    rows_scratch = pltpu.VMEM((ITEM, HD), F32)
    q = queries.reshape(STEPS, PER * HD)

    spread = call(
        spread_kernel, "spread", struct((far, ITEM, HD), BF16), [VMEM], VMEM, [rows_scratch]
    )(q)
    chosen = selected[:, 0, :].T
    here = call(
        pack_kernel,
        "pack",
        struct((2 * tokens + FLAG, HD), BF16),
        [ANY] * 3,
        VMEM,
        [pltpu.VMEM(chosen.shape, jnp.int32), pltpu.SemaphoreType.DMA((3,))],
        vmem=62,
    )(prompt_keys, prompt_values, chosen)
    gathered = swap(spread, FAR)
    packs = [
        here,
        lax.ppermute(here, "yl", [(0, 1), (1, 0)]),
        lax.ppermute(here, "zl", [(0, 1), (1, 0)]),
        lax.ppermute(here, NEAR, [(0, 3), (1, 2), (2, 1), (3, 0)]),
    ]
    own, own_log = call(
        own_kernel,
        "own",
        (struct((ITEM, HD), F32), struct((8, HD), F32)),
        [VMEM] * 5 + [SMEM],
        (VMEM, VMEM),
        [rows_scratch],
        flops=10**6,
        moved=3 * 10**5,
    )(q, cache_keys[0], cache_values[0], new_keys[:, 0], new_values[:, 0], positions)
    partial = call(
        prompt_kernel,
        "prompt",
        struct((far, ITEM + STAT, HD), BF16),
        [SMEM, ANY] + [VMEM] * 5,
        VMEM,
        [pltpu.VMEM((2 * HD, 4 * tokens), BF16)],
    )(place, own, gathered, *packs)
    received = swap(partial, FAR)
    attended = call(
        combine_kernel, "combine", struct((samples, ITEM, HD), BF16), [VMEM] * 3, VMEM
    )(received, own, own_log)
    every = swap(attended, CTX)
    product = call(
        project_kernel,
        "project",
        struct((heads, STEPS * samples // heads, columns), F32),
        [VMEM] * 2,
        VMEM,
        [pltpu.VMEM((samples * ITEM, HD), F32)],
    )(every, out_weight)
    terms = swap(product, "head")
    return call(
        sum_kernel, "sum", struct((STEPS, samples // heads, columns), BF16), [VMEM], VMEM
    )(terms)


def solution(mesh):
    fine = Mesh(mesh.devices.reshape(4, 2, 4, 2, 8), (*CTX, "head"))
    placed = (
        P(None, CTX, "head"),
        P(CTX, "head"),
        P(CTX, "head"),
        P(None, "head", CTX),
        P(CTX, None, "head"),
        P(CTX, None, "head"),
        P(None, CTX, "head"),
        P(None, CTX, "head"),
        P(CTX),
        P("head", CTX),
    )
    return jax.shard_map(
        shards, mesh=fine, in_specs=placed, out_specs=P(None, "head", CTX), check_vma=False
    )
```

```python
import math

import jax
import jax.numpy as jnp
from jax import lax
from jax.experimental import pallas as pl
from jax.experimental.pallas import tpu as pltpu
from jax.sharding import PartitionSpec as P

HD = 128
KVH = 8
PER = 16
BLOCK = 64
STEPS = 2
ITEM = STEPS * PER
STAT = 8
FLAG = 16
NEGATIVE = -1e30
SCALE = math.log2(math.e) / math.sqrt(HD)
TILE = 4
BOTH = ("ctx", "head")
SIDE = 8
CORES = 2
GAP = 2

VMEM = pl.BlockSpec(memory_space=pltpu.VMEM)
SMEM = pl.BlockSpec(memory_space=pltpu.SMEM)
ANY = pl.BlockSpec(memory_space=pl.ANY)
F32 = jnp.float32
BF16 = jnp.bfloat16


def dot(a, b):
    return lax.dot_general(a, b, (((1,), (0,)), ((), ())), preferred_element_type=F32)


def dot_t(a, b):
    return lax.dot_general(a, b, (((1,), (1,)), ((), ())), preferred_element_type=F32)


def iota(shape, dim):
    return lax.broadcasted_iota(jnp.int32, shape, dim)


def item_rows(q_ref, rows_ref):
    whole = q_ref[...].astype(F32)
    for step in range(STEPS):
        for head in range(PER):
            row = step * PER + head
            rows_ref[row : row + 1, :] = whole[step : step + 1, head * HD : (head + 1) * HD]
    return rows_ref[...]


def to_lanes(column, count):
    shape = (count, ITEM, HD)
    pick = iota(shape, 1) == iota(shape, 2) % ITEM
    return jnp.sum(jnp.where(pick, column.reshape(shape), 0.0), axis=1)


def spread_kernel(q_ref, out_ref, rows_ref):
    rows = item_rows(q_ref, rows_ref).astype(BF16)
    out_ref[...] = jnp.broadcast_to(rows[None], out_ref.shape)


def pack_kernel(k_hbm, v_hbm, sel_hbm, out_ref, sel_ref, sems):
    tokens = k_hbm.shape[0]
    copies = [
        pltpu.make_async_copy(sel_hbm, sel_ref, sems.at[0]),
        pltpu.make_async_copy(k_hbm, out_ref.at[:tokens], sems.at[1]),
        pltpu.make_async_copy(v_hbm, out_ref.at[tokens : 2 * tokens], sems.at[2]),
    ]
    for copy in copies:
        copy.start()
    copies[0].wait()
    slots, samples = sel_ref.shape
    number = iota((FLAG, samples), 0)
    bias = jnp.full((FLAG, samples), NEGATIVE, F32)
    for slot in range(slots):
        bias = jnp.where(sel_ref[slot : slot + 1, :] == number, 0.0, bias)
    bias = jnp.concatenate([bias, jnp.zeros((FLAG, HD - samples), F32)], axis=1)
    out_ref[2 * tokens :, :] = bias.astype(BF16)
    for copy in copies[1:]:
        copy.wait()


def own_kernel(q_ref, ck_ref, cv_ref, nk_ref, nv_ref, pos_ref, out_ref, log_ref, rows_ref):
    rows = item_rows(q_ref, rows_ref)
    slots = ck_ref.shape[0]
    scores = dot_t(rows.astype(BF16), ck_ref[...]) * SCALE
    alive = iota((ITEM, slots), 1) < pos_ref[0]
    scores = jnp.where(alive, scores, NEGATIVE)
    top = jnp.max(scores, axis=1, keepdims=True)
    step = iota((ITEM, 1), 0) // PER
    new_scores = []
    for token in range(STEPS):
        key = nk_ref[token : token + 1, :].astype(F32)
        score = jnp.sum(rows * key, axis=1, keepdims=True) * SCALE
        score = jnp.where(step >= token, score, NEGATIVE)
        new_scores.append(score)
        top = jnp.maximum(top, score)
    weights = jnp.where(alive, jnp.exp2(scores - top), 0.0)
    mass = jnp.sum(weights, axis=1, keepdims=True)
    total = dot(weights.astype(BF16), cv_ref[...])
    for token in range(STEPS):
        weight = jnp.where(step >= token, jnp.exp2(new_scores[token] - top), 0.0)
        mass = mass + weight
        value = nv_ref[token : token + 1, :].astype(F32)
        total = total + weight.astype(BF16).astype(F32) * value
    out_ref[...] = total / mass
    log_mass = jnp.broadcast_to(top + jnp.log2(mass), (ITEM, HD))
    log_ref[...] = jnp.broadcast_to(to_lanes(log_mass, 1), log_ref.shape)


def prompt_kernel(place_ref, own_ref, q_ref, *refs):
    *pack_refs, out_ref, keys_ref = refs
    samples = q_ref.shape[0]
    tokens = (pack_refs[0].shape[0] - FLAG) // 2
    widen = iota((FLAG, tokens), 1) // BLOCK == iota((FLAG, tokens), 0)
    widen = widen.astype(F32).astype(BF16)
    for index, ref in enumerate(pack_refs):
        place = slice(index * tokens, (index + 1) * tokens)
        keys_ref[:HD, place] = ref[:tokens, :].T
        bias = lax.dot_general(
            ref[2 * tokens :, :], widen, (((0,), (0,)), ((), ())), preferred_element_type=F32
        )
        keys_ref[HD:, place] = bias.astype(BF16)
    ones = jnp.ones((tokens, HD), BF16)
    count = TILE * ITEM
    number = iota((count, HD), 0) // ITEM
    lane = iota((count, HD), 1) - place_ref[1]
    for first in range(0, samples, TILE):
        here = slice(first, first + TILE)
        q = q_ref[here].reshape(count, HD)
        ring, near = (first + number) // GAP, (first + number) % GAP
        sample = jnp.where(place_ref[0] == 0, ring * SIDE + near, near * SIDE + ring)
        mine = lane == sample
        q = jnp.concatenate([q, mine.astype(F32).astype(BF16)], axis=1)
        scores = []
        for index in range(len(pack_refs)):
            scores.append(dot(q, keys_ref[:, index * tokens : (index + 1) * tokens]))
        top = scores[0]
        for score in scores[1:]:
            top = jnp.maximum(top, score)
        top = jnp.max(top, axis=1, keepdims=True)
        total = jnp.zeros((count, 2 * HD), F32)
        for score, ref in zip(scores, pack_refs):
            weights = jnp.exp2((score - top) * SCALE).astype(BF16)
            values = jnp.concatenate([ref[tokens : 2 * tokens, :], ones], axis=1)
            total = total + dot(weights, values)
        mass = total[:, HD:]
        out_ref[here, :ITEM, :] = (total[:, :HD] / mass).astype(BF16).reshape(TILE, ITEM, HD)
        log_mass = to_lanes(top * SCALE + jnp.log2(mass), TILE)
        high = log_mass.astype(BF16).astype(F32)
        rest = log_mass - high
        middle = rest.astype(BF16).astype(F32)
        low = rest - middle
        shape = (TILE, STAT, HD)
        row = iota(shape, 1)
        stat = jnp.where(row == 0, jnp.broadcast_to(high[:, None, :], shape), 0.0)
        stat = jnp.where(row == 1, jnp.broadcast_to(middle[:, None, :], shape), stat)
        stat = jnp.where(row == 2, jnp.broadcast_to(low[:, None, :], shape), stat)
        out_ref[here, ITEM:, :] = stat.astype(BF16)


def combine_kernel(part_ref, own_ref, own_log_ref, out_ref):
    shards = part_ref.shape[0]
    log_mass = jnp.sum(part_ref[:, ITEM:, :].astype(F32), axis=1)
    own_log = own_log_ref[0:1, :]
    best = jnp.maximum(jnp.max(log_mass, axis=0, keepdims=True), own_log)
    weights = jnp.exp2(log_mass - best)
    own_weight = jnp.exp2(own_log - best)
    whole = jnp.sum(weights, axis=0, keepdims=True) + own_weight
    weights = weights / whole
    own_weight = own_weight / whole
    per_lane = HD // ITEM
    groups = shards // per_lane
    lane = iota((groups, HD), 1) // ITEM
    packed = jnp.zeros((groups, HD), F32)
    for turn in range(per_lane):
        packed = jnp.where(lane == turn, weights[turn * groups : (turn + 1) * groups], packed)
    pick = iota((ITEM, HD), 0) == iota((ITEM, HD), 1) % ITEM
    factors = []
    rows = []
    for group in range(groups):
        factors.append(jnp.where(pick, packed[group : group + 1], 0.0))
        for turn in range(per_lane):
            rows.append(part_ref[group + turn * groups, :ITEM, :])
    factor = jnp.concatenate(factors, axis=1)
    high = factor.astype(BF16)
    low = (factor - high.astype(F32)).astype(BF16)
    total = dot(jnp.concatenate([high, low], axis=0), jnp.concatenate(rows, axis=0))
    total = total[:ITEM] + total[ITEM:]
    own_column = jnp.sum(
        jnp.where(iota((ITEM, HD), 0) == iota((ITEM, HD), 1), own_weight, 0.0),
        axis=1,
        keepdims=True,
    )
    attended = (total + own_column * own_ref[...]).astype(BF16)
    out_ref[...] = jnp.broadcast_to(attended[None], out_ref.shape)


def project_kernel(x_ref, w_ref, out_ref, rows_ref):
    samples = x_ref.shape[0]
    parts = out_ref.shape[0]
    per_part = samples // parts
    rows_ref[...] = x_ref[...].reshape(samples * ITEM, HD).astype(F32)
    columns = []
    for head in range(PER):
        pieces = [
            rows_ref[pl.ds(step * PER + head, samples, stride=ITEM), :] for step in range(STEPS)
        ]
        columns.append(jnp.concatenate(pieces, axis=0).astype(BF16))
    product = dot(jnp.concatenate(columns, axis=1), w_ref[...])
    for part in range(parts):
        pieces = [
            product[step * samples + part * per_part : step * samples + (part + 1) * per_part]
            for step in range(STEPS)
        ]
        out_ref[part] = jnp.concatenate(pieces, axis=0).astype(out_ref.dtype)


def sum_kernel(x_ref, out_ref):
    total = jnp.sum(x_ref[...].astype(F32), axis=0)
    out_ref[...] = total.reshape(out_ref.shape).astype(BF16)


def call(
    kernel, name, out_shape, in_specs, out_specs, scratch=(), flops=0, moved=0, vmem=24
):
    return pl.pallas_call(
        kernel,
        name=name,
        out_shape=out_shape,
        in_specs=in_specs,
        out_specs=out_specs,
        scratch_shapes=scratch,
        compiler_params=pltpu.CompilerParams(vmem_limit_bytes=vmem * 1024 * 1024),
        cost_estimate=pl.CostEstimate(flops=flops, bytes_accessed=moved, transcendentals=0),
    )


def swap(array, axes, groups=None):
    return lax.all_to_all(
        array, axes, split_axis=0, concat_axis=0, axis_index_groups=groups, tiled=True
    )


def device(z, y, head):
    return (z % SIDE * SIDE + y % SIDE) * KVH + head


def far_groups():
    groups = []
    for head in range(KVH):
        for first in range(0, SIDE, GAP):
            group = []
            for ring in range(SIDE):
                for near in range(first, first + GAP):
                    z, y = (ring, near) if head % CORES == 0 else (near, ring)
                    group.append(device(z, y, head))
            groups.append(group)
    return groups


def hops(count):
    pairs = []
    for head in range(KVH):
        for z in range(SIDE):
            for y in range(SIDE):
                move = count * GAP
                target = (z, y + move) if head % CORES == 0 else (z + move, y)
                pairs.append((device(z, y, head), device(*target, head)))
    return pairs


def shards(
    queries,
    prompt_keys,
    prompt_values,
    selected,
    cache_keys,
    cache_values,
    new_keys,
    new_values,
    positions,
    out_weight,
):
    struct = jax.ShapeDtypeStruct
    samples = lax.axis_size("ctx")
    far = SIDE * GAP
    heads = lax.axis_size("head")
    tokens = prompt_keys.shape[0]
    columns = out_weight.shape[1]
    ctx = lax.axis_index("ctx")
    odd = lax.axis_index("head") % CORES
    start = jnp.where(odd == 0, ctx % SIDE // GAP * GAP, ctx // SIDE // GAP * GAP * SIDE)
    place = jnp.stack([odd, start]).astype(jnp.int32)
    groups = far_groups()
    rows_scratch = pltpu.VMEM((ITEM, HD), F32)
    q = queries.reshape(STEPS, PER * HD)

    spread = call(
        spread_kernel, "spread", struct((far, ITEM, HD), BF16), [VMEM], VMEM, [rows_scratch]
    )(q)
    chosen = selected[:, 0, :].T
    here = call(
        pack_kernel,
        "pack",
        struct((2 * tokens + FLAG, HD), BF16),
        [ANY] * 3,
        VMEM,
        [pltpu.VMEM(chosen.shape, jnp.int32), pltpu.SemaphoreType.DMA((3,))],
        vmem=62,
    )(prompt_keys, prompt_values, chosen)
    gathered = swap(spread, BOTH, groups)
    packs = [here]
    for count in range(1, SIDE // GAP):
        packs.append(lax.ppermute(here, BOTH, hops(count)))
    own, own_log = call(
        own_kernel,
        "own",
        (struct((ITEM, HD), F32), struct((8, HD), F32)),
        [VMEM] * 5 + [SMEM],
        (VMEM, VMEM),
        [rows_scratch],
        flops=10**6,
        moved=3 * 10**5,
    )(q, cache_keys[0], cache_values[0], new_keys[:, 0], new_values[:, 0], positions)
    partial = call(
        prompt_kernel,
        "prompt",
        struct((far, ITEM + STAT, HD), BF16),
        [SMEM, ANY] + [VMEM] * 5,
        VMEM,
        [pltpu.VMEM((2 * HD, 4 * tokens), BF16)],
    )(place, own, gathered, *packs)
    received = swap(partial, BOTH, groups)
    attended = call(
        combine_kernel, "combine", struct((samples, ITEM, HD), BF16), [VMEM] * 3, VMEM
    )(received, own, own_log)
    every = swap(attended, "ctx")
    product = call(
        project_kernel,
        "project",
        struct((heads, STEPS * samples // heads, columns), F32),
        [VMEM] * 2,
        VMEM,
        [pltpu.VMEM((samples * ITEM, HD), F32)],
    )(every, out_weight)
    terms = swap(product, "head")
    return call(
        sum_kernel, "sum", struct((STEPS, samples // heads, columns), BF16), [VMEM], VMEM
    )(terms)


def solution(mesh):
    placed = (
        P(None, "ctx", "head"),
        P("ctx", "head"),
        P("ctx", "head"),
        P(None, "head", "ctx"),
        P("ctx", None, "head"),
        P("ctx", None, "head"),
        P(None, "ctx", "head"),
        P(None, "ctx", "head"),
        P("ctx"),
        P("head", "ctx"),
    )
    return jax.shard_map(
        shards, mesh=mesh, in_specs=placed, out_specs=P(None, "head", "ctx"), check_vma=False
    )
```

```python
import math

import jax
import jax.numpy as jnp
from jax import lax
from jax.experimental import pallas as pl
from jax.experimental.pallas import tpu as pltpu
from jax.sharding import PartitionSpec as P

HD = 128
KVH = 8
PER = 16
BLOCK = 64
STEPS = 2
ITEM = STEPS * PER
STAT = 8
FLAG = 16
NEGATIVE = -1e30
SCALE = math.log2(math.e) / math.sqrt(HD)
TILE = 4
BOTH = ("ctx", "head")
SIDE = 8
CORES = 2
GAP = 2

VMEM = pl.BlockSpec(memory_space=pltpu.VMEM)
SMEM = pl.BlockSpec(memory_space=pltpu.SMEM)
ANY = pl.BlockSpec(memory_space=pl.ANY)
F32 = jnp.float32
BF16 = jnp.bfloat16


def dot(a, b):
    return lax.dot_general(a, b, (((1,), (0,)), ((), ())), preferred_element_type=F32)


def dot_t(a, b):
    return lax.dot_general(a, b, (((1,), (1,)), ((), ())), preferred_element_type=F32)


def iota(shape, dim):
    return lax.broadcasted_iota(jnp.int32, shape, dim)


def item_rows(q_ref, rows_ref):
    whole = q_ref[...].astype(F32)
    for step in range(STEPS):
        for head in range(PER):
            row = step * PER + head
            rows_ref[row : row + 1, :] = whole[step : step + 1, head * HD : (head + 1) * HD]
    return rows_ref[...]


def to_lanes(column, count):
    shape = (count, ITEM, HD)
    pick = iota(shape, 1) == iota(shape, 2) % ITEM
    return jnp.sum(jnp.where(pick, column.reshape(shape), 0.0), axis=1)


def pack_kernel(
    q_hbm, k_hbm, v_hbm, sel_hbm, spread_ref, out_ref, q_ref, sel_ref, rows_ref, sems
):
    tokens = k_hbm.shape[0]
    copies = [
        pltpu.make_async_copy(q_hbm, q_ref, sems.at[0]),
        pltpu.make_async_copy(sel_hbm, sel_ref, sems.at[1]),
        pltpu.make_async_copy(k_hbm, out_ref.at[:tokens], sems.at[2]),
        pltpu.make_async_copy(v_hbm, out_ref.at[tokens : 2 * tokens], sems.at[3]),
    ]
    for copy in copies:
        copy.start()
    copies[0].wait()
    rows = item_rows(q_ref, rows_ref).astype(BF16)
    spread_ref[...] = jnp.broadcast_to(rows[None], spread_ref.shape)
    copies[1].wait()
    slots, samples = sel_ref.shape
    number = iota((FLAG, samples), 0)
    bias = jnp.full((FLAG, samples), NEGATIVE, F32)
    for slot in range(slots):
        bias = jnp.where(sel_ref[slot : slot + 1, :] == number, 0.0, bias)
    bias = jnp.concatenate([bias, jnp.zeros((FLAG, HD - samples), F32)], axis=1)
    out_ref[2 * tokens :, :] = bias.astype(BF16)
    for copy in copies[2:]:
        copy.wait()


def own_kernel(q_ref, ck_ref, cv_ref, nk_ref, nv_ref, pos_ref, out_ref, log_ref, rows_ref):
    rows = item_rows(q_ref, rows_ref)
    slots = ck_ref.shape[0]
    scores = dot_t(rows.astype(BF16), ck_ref[...]) * SCALE
    alive = iota((ITEM, slots), 1) < pos_ref[0]
    scores = jnp.where(alive, scores, NEGATIVE)
    top = jnp.max(scores, axis=1, keepdims=True)
    step = iota((ITEM, 1), 0) // PER
    new_scores = []
    for token in range(STEPS):
        key = nk_ref[token : token + 1, :].astype(F32)
        score = jnp.sum(rows * key, axis=1, keepdims=True) * SCALE
        score = jnp.where(step >= token, score, NEGATIVE)
        new_scores.append(score)
        top = jnp.maximum(top, score)
    weights = jnp.where(alive, jnp.exp2(scores - top), 0.0)
    mass = jnp.sum(weights, axis=1, keepdims=True)
    total = dot(weights.astype(BF16), cv_ref[...])
    for token in range(STEPS):
        weight = jnp.where(step >= token, jnp.exp2(new_scores[token] - top), 0.0)
        mass = mass + weight
        value = nv_ref[token : token + 1, :].astype(F32)
        total = total + weight.astype(BF16).astype(F32) * value
    out_ref[...] = total / mass
    log_mass = jnp.broadcast_to(top + jnp.log2(mass), (ITEM, HD))
    log_ref[...] = jnp.broadcast_to(to_lanes(log_mass, 1), log_ref.shape)


def prompt_kernel(place_ref, own_ref, q_ref, *refs):
    *pack_refs, out_ref, keys_ref = refs
    samples = q_ref.shape[0]
    tokens = (pack_refs[0].shape[0] - FLAG) // 2
    widen = iota((FLAG, tokens), 1) // BLOCK == iota((FLAG, tokens), 0)
    widen = widen.astype(F32).astype(BF16)
    for index, ref in enumerate(pack_refs):
        place = slice(index * tokens, (index + 1) * tokens)
        keys_ref[:HD, place] = ref[:tokens, :].T
        bias = lax.dot_general(
            ref[2 * tokens :, :], widen, (((0,), (0,)), ((), ())), preferred_element_type=F32
        )
        keys_ref[HD:, place] = bias.astype(BF16)
    ones = jnp.ones((tokens, HD), BF16)
    count = TILE * ITEM
    number = iota((count, HD), 0) // ITEM
    ring, near = number // GAP, number % GAP
    odd, start = place_ref[0] // (SIDE * SIDE), place_ref[0] % (SIDE * SIDE)
    sample = jnp.where(odd == 0, ring * SIDE + near, near * SIDE + ring)
    lane = iota((count, HD), 1) - sample
    for first in range(0, samples, TILE):
        here = slice(first, first + TILE)
        q = q_ref[here].reshape(count, HD)
        mine = lane == start + first // GAP * jnp.where(odd == 0, SIDE, 1)
        q = jnp.concatenate([q, mine.astype(F32).astype(BF16)], axis=1)
        scores = []
        for index in range(len(pack_refs)):
            scores.append(dot(q, keys_ref[:, index * tokens : (index + 1) * tokens]))
        top = scores[0]
        for score in scores[1:]:
            top = jnp.maximum(top, score)
        top = jnp.max(top, axis=1, keepdims=True)
        total = jnp.zeros((count, 2 * HD), F32)
        for score, ref in zip(scores, pack_refs):
            weights = jnp.exp2((score - top) * SCALE).astype(BF16)
            values = jnp.concatenate([ref[tokens : 2 * tokens, :], ones], axis=1)
            total = total + dot(weights, values)
        mass = total[:, HD:]
        out_ref[here, :ITEM, :] = (total[:, :HD] / mass).astype(BF16).reshape(TILE, ITEM, HD)
        log_mass = to_lanes(top * SCALE + jnp.log2(mass), TILE)
        high = log_mass.astype(BF16).astype(F32)
        rest = log_mass - high
        middle = rest.astype(BF16).astype(F32)
        low = rest - middle
        shape = (TILE, STAT, HD)
        row = iota(shape, 1)
        stat = jnp.where(row == 0, jnp.broadcast_to(high[:, None, :], shape), 0.0)
        stat = jnp.where(row == 1, jnp.broadcast_to(middle[:, None, :], shape), stat)
        stat = jnp.where(row == 2, jnp.broadcast_to(low[:, None, :], shape), stat)
        out_ref[here, ITEM:, :] = stat.astype(BF16)


def combine_kernel(part_ref, own_ref, own_log_ref, out_ref):
    shards = part_ref.shape[0]
    log_mass = jnp.sum(part_ref[:, ITEM:, :].astype(F32), axis=1)
    own_log = own_log_ref[0:1, :]
    best = jnp.maximum(jnp.max(log_mass, axis=0, keepdims=True), own_log)
    weights = jnp.exp2(log_mass - best)
    own_weight = jnp.exp2(own_log - best)
    whole = jnp.sum(weights, axis=0, keepdims=True) + own_weight
    weights = weights / whole
    own_weight = own_weight / whole
    per_lane = HD // ITEM
    groups = shards // per_lane
    lane = iota((groups, HD), 1) // ITEM
    packed = jnp.zeros((groups, HD), F32)
    for turn in range(per_lane):
        packed = jnp.where(lane == turn, weights[turn * groups : (turn + 1) * groups], packed)
    pick = iota((ITEM, HD), 0) == iota((ITEM, HD), 1) % ITEM
    factors = []
    rows = []
    for group in range(groups):
        factors.append(jnp.where(pick, packed[group : group + 1], 0.0))
        for turn in range(per_lane):
            rows.append(part_ref[group + turn * groups, :ITEM, :])
    factor = jnp.concatenate(factors, axis=1)
    high = factor.astype(BF16)
    low = (factor - high.astype(F32)).astype(BF16)
    total = dot(jnp.concatenate([high, low], axis=0), jnp.concatenate(rows, axis=0))
    total = total[:ITEM] + total[ITEM:]
    own_column = jnp.sum(
        jnp.where(iota((ITEM, HD), 0) == iota((ITEM, HD), 1), own_weight, 0.0),
        axis=1,
        keepdims=True,
    )
    attended = (total + own_column * own_ref[...]).astype(BF16)
    out_ref[...] = jnp.broadcast_to(attended[None], out_ref.shape)


def project_kernel(x_ref, w_ref, out_ref, rows_ref):
    samples = x_ref.shape[0]
    parts = out_ref.shape[0]
    per_part = samples // parts
    rows_ref[...] = x_ref[...].reshape(samples * ITEM, HD).astype(F32)
    columns = []
    for head in range(PER):
        pieces = [
            rows_ref[pl.ds(step * PER + head, samples, stride=ITEM), :] for step in range(STEPS)
        ]
        columns.append(jnp.concatenate(pieces, axis=0).astype(BF16))
    product = dot(jnp.concatenate(columns, axis=1), w_ref[...])
    for part in range(parts):
        pieces = [
            product[step * samples + part * per_part : step * samples + (part + 1) * per_part]
            for step in range(STEPS)
        ]
        out_ref[part] = jnp.concatenate(pieces, axis=0).astype(out_ref.dtype)


def sum_kernel(x_ref, out_ref):
    total = jnp.sum(x_ref[...].astype(F32), axis=0)
    out_ref[...] = total.reshape(out_ref.shape).astype(BF16)


def call(
    kernel, name, out_shape, in_specs, out_specs, scratch=(), flops=0, moved=0, vmem=24
):
    return pl.pallas_call(
        kernel,
        name=name,
        out_shape=out_shape,
        in_specs=in_specs,
        out_specs=out_specs,
        scratch_shapes=scratch,
        compiler_params=pltpu.CompilerParams(vmem_limit_bytes=vmem * 1024 * 1024),
        cost_estimate=pl.CostEstimate(flops=flops, bytes_accessed=moved, transcendentals=0),
    )


def swap(array, axes, groups=None):
    return lax.all_to_all(
        array, axes, split_axis=0, concat_axis=0, axis_index_groups=groups, tiled=True
    )


def device(z, y, head):
    return (z % SIDE * SIDE + y % SIDE) * KVH + head


def far_groups():
    groups = []
    for head in range(KVH):
        for first in range(0, SIDE, GAP):
            group = []
            for ring in range(SIDE):
                for near in range(first, first + GAP):
                    z, y = (ring, near) if head % CORES == 0 else (near, ring)
                    group.append(device(z, y, head))
            groups.append(group)
    return groups


def hops(count):
    pairs = []
    for head in range(KVH):
        for z in range(SIDE):
            for y in range(SIDE):
                move = count * GAP
                target = (z, y + move) if head % CORES == 0 else (z + move, y)
                pairs.append((device(z, y, head), device(*target, head)))
    return pairs


def shards(
    queries,
    prompt_keys,
    prompt_values,
    selected,
    cache_keys,
    cache_values,
    new_keys,
    new_values,
    positions,
    out_weight,
):
    struct = jax.ShapeDtypeStruct
    samples = lax.axis_size("ctx")
    far = SIDE * GAP
    heads = lax.axis_size("head")
    tokens = prompt_keys.shape[0]
    columns = out_weight.shape[1]
    ctx = lax.axis_index("ctx")
    odd = lax.axis_index("head") % CORES
    start = jnp.where(odd == 0, ctx % SIDE // GAP * GAP, ctx // SIDE // GAP * GAP * SIDE)
    place = (odd * (SIDE * SIDE) + start).astype(jnp.int32).reshape(1)
    groups = far_groups()
    rows_scratch = pltpu.VMEM((ITEM, HD), F32)
    q = queries.reshape(STEPS, PER * HD)

    chosen = selected[:, 0, :].T
    spread, here = call(
        pack_kernel,
        "pack",
        (struct((far, ITEM, HD), BF16), struct((2 * tokens + FLAG, HD), BF16)),
        [ANY] * 4,
        (VMEM, VMEM),
        [
            pltpu.VMEM(q.shape, BF16),
            pltpu.VMEM(chosen.shape, jnp.int32),
            rows_scratch,
            pltpu.SemaphoreType.DMA((4,)),
        ],
        vmem=62,
    )(q, prompt_keys, prompt_values, chosen)
    gathered = swap(spread, BOTH, groups)
    packs = [here]
    for count in range(1, SIDE // GAP):
        packs.append(lax.ppermute(here, BOTH, hops(count)))
    own, own_log = call(
        own_kernel,
        "own",
        (struct((ITEM, HD), F32), struct((8, HD), F32)),
        [VMEM] * 5 + [SMEM],
        (VMEM, VMEM),
        [rows_scratch],
        flops=10**6,
        moved=3 * 10**5,
    )(q, cache_keys[0], cache_values[0], new_keys[:, 0], new_values[:, 0], positions)
    partial = call(
        prompt_kernel,
        "prompt",
        struct((far, ITEM + STAT, HD), BF16),
        [SMEM, ANY] + [VMEM] * 5,
        VMEM,
        [pltpu.VMEM((2 * HD, 4 * tokens), BF16)],
    )(place, own, gathered, *packs)
    received = swap(partial, BOTH, groups)
    attended = call(
        combine_kernel, "combine", struct((samples, ITEM, HD), BF16), [VMEM] * 3, VMEM
    )(received, own, own_log)
    every = swap(attended, "ctx")
    product = call(
        project_kernel,
        "project",
        struct((heads, STEPS * samples // heads, columns), F32),
        [VMEM] * 2,
        VMEM,
        [pltpu.VMEM((samples * ITEM, HD), F32)],
    )(every, out_weight)
    terms = swap(product, "head")
    return call(
        sum_kernel, "sum", struct((STEPS, samples // heads, columns), BF16), [VMEM], VMEM
    )(terms)


def solution(mesh):
    placed = (
        P(None, "ctx", "head"),
        P("ctx", "head"),
        P("ctx", "head"),
        P(None, "head", "ctx"),
        P("ctx", None, "head"),
        P("ctx", None, "head"),
        P(None, "ctx", "head"),
        P(None, "ctx", "head"),
        P("ctx"),
        P("head", "ctx"),
    )
    return jax.shard_map(
        shards, mesh=mesh, in_specs=placed, out_specs=P(None, "head", "ctx"), check_vma=False
    )
```

```python
import math

import jax
import jax.numpy as jnp
from jax import lax
from jax.experimental import pallas as pl
from jax.experimental.pallas import tpu as pltpu
from jax.sharding import PartitionSpec as P

HD = 128
KVH = 8
PER = 16
BLOCK = 64
STEPS = 2
ITEM = STEPS * PER
STAT = 8
FLAG = 16
NEGATIVE = -1e30
SCALE = math.log2(math.e) / math.sqrt(HD)
TILE = 4
BOTH = ("ctx", "head")
SIDE = 8
CORES = 2
GAP = 2

VMEM = pl.BlockSpec(memory_space=pltpu.VMEM)
SMEM = pl.BlockSpec(memory_space=pltpu.SMEM)
ANY = pl.BlockSpec(memory_space=pl.ANY)
F32 = jnp.float32
BF16 = jnp.bfloat16


def dot(a, b):
    return lax.dot_general(a, b, (((1,), (0,)), ((), ())), preferred_element_type=F32)


def dot_t(a, b):
    return lax.dot_general(a, b, (((1,), (1,)), ((), ())), preferred_element_type=F32)


def iota(shape, dim):
    return lax.broadcasted_iota(jnp.int32, shape, dim)


def item_rows(q_ref, rows_ref):
    whole = q_ref[...].astype(F32)
    for step in range(STEPS):
        for head in range(PER):
            row = step * PER + head
            rows_ref[row : row + 1, :] = whole[step : step + 1, head * HD : (head + 1) * HD]
    return rows_ref[...]


def to_lanes(column, count):
    shape = (count, ITEM, HD)
    pick = iota(shape, 1) == iota(shape, 2) % ITEM
    return jnp.sum(jnp.where(pick, column.reshape(shape), 0.0), axis=1)


def pack_kernel(
    q_hbm, k_hbm, v_hbm, sel_hbm, spread_ref, out_ref, q_ref, sel_ref, rows_ref, sems
):
    tokens = k_hbm.shape[0]
    copies = [
        pltpu.make_async_copy(q_hbm, q_ref, sems.at[0]),
        pltpu.make_async_copy(sel_hbm, sel_ref, sems.at[1]),
        pltpu.make_async_copy(k_hbm, out_ref.at[:tokens], sems.at[2]),
        pltpu.make_async_copy(v_hbm, out_ref.at[tokens : 2 * tokens], sems.at[3]),
    ]
    for copy in copies:
        copy.start()
    copies[0].wait()
    rows = item_rows(q_ref, rows_ref).astype(BF16)
    spread_ref[...] = jnp.broadcast_to(rows[None], spread_ref.shape)
    copies[1].wait()
    slots, samples = sel_ref.shape
    number = iota((FLAG, samples), 0)
    bias = jnp.full((FLAG, samples), NEGATIVE, F32)
    for slot in range(slots):
        bias = jnp.where(sel_ref[slot : slot + 1, :] == number, 0.0, bias)
    bias = jnp.concatenate([bias, jnp.zeros((FLAG, HD - samples), F32)], axis=1)
    out_ref[2 * tokens :, :] = bias.astype(BF16)
    for copy in copies[2:]:
        copy.wait()


def own_kernel(q_ref, ck_ref, cv_ref, nk_ref, nv_ref, pos_ref, out_ref, log_ref, rows_ref):
    rows = item_rows(q_ref, rows_ref)
    slots = ck_ref.shape[0]
    scores = dot_t(rows.astype(BF16), ck_ref[...]) * SCALE
    alive = iota((ITEM, slots), 1) < pos_ref[0]
    scores = jnp.where(alive, scores, NEGATIVE)
    top = jnp.max(scores, axis=1, keepdims=True)
    step = iota((ITEM, 1), 0) // PER
    new_scores = []
    for token in range(STEPS):
        key = nk_ref[token : token + 1, :].astype(F32)
        score = jnp.sum(rows * key, axis=1, keepdims=True) * SCALE
        score = jnp.where(step >= token, score, NEGATIVE)
        new_scores.append(score)
        top = jnp.maximum(top, score)
    weights = jnp.where(alive, jnp.exp2(scores - top), 0.0)
    mass = jnp.sum(weights, axis=1, keepdims=True)
    total = dot(weights.astype(BF16), cv_ref[...])
    for token in range(STEPS):
        weight = jnp.where(step >= token, jnp.exp2(new_scores[token] - top), 0.0)
        mass = mass + weight
        value = nv_ref[token : token + 1, :].astype(F32)
        total = total + weight.astype(BF16).astype(F32) * value
    out_ref[...] = total / mass
    log_mass = jnp.broadcast_to(top + jnp.log2(mass), (ITEM, HD))
    log_ref[...] = jnp.broadcast_to(to_lanes(log_mass, 1), log_ref.shape)


def prompt_kernel(place_ref, own_ref, q_ref, *refs):
    *pack_refs, out_ref, keys_ref = refs
    samples = q_ref.shape[0]
    tokens = (pack_refs[0].shape[0] - FLAG) // 2
    widen = iota((FLAG, tokens), 1) // BLOCK == iota((FLAG, tokens), 0)
    widen = widen.astype(F32).astype(BF16)
    for index, ref in enumerate(pack_refs):
        place = slice(index * tokens, (index + 1) * tokens)
        keys_ref[:HD, place] = ref[:tokens, :].T
        bias = lax.dot_general(
            ref[2 * tokens :, :], widen, (((0,), (0,)), ((), ())), preferred_element_type=F32
        )
        keys_ref[HD:, place] = bias.astype(BF16)
    ones = jnp.ones((tokens, HD), BF16)
    count = TILE * ITEM
    number = iota((count, HD), 0) // ITEM
    ring, near = number // GAP, number % GAP
    odd, start = place_ref[0] // (SIDE * SIDE), place_ref[0] % (SIDE * SIDE)
    sample = jnp.where(odd == 0, ring * SIDE + near, near * SIDE + ring)
    lane = iota((count, HD), 1) - sample
    for first in range(0, samples, TILE):
        here = slice(first, first + TILE)
        q = q_ref[here].reshape(count, HD)
        mine = lane == start + first // GAP * jnp.where(odd == 0, SIDE, 1)
        q = jnp.concatenate([q, mine.astype(F32).astype(BF16)], axis=1)
        scores = []
        for index in range(len(pack_refs)):
            scores.append(dot(q, keys_ref[:, index * tokens : (index + 1) * tokens]))
        top = scores[0]
        for score in scores[1:]:
            top = jnp.maximum(top, score)
        top = jnp.max(top, axis=1, keepdims=True)
        total = jnp.zeros((count, 2 * HD), F32)
        for score, ref in zip(scores, pack_refs):
            weights = jnp.exp2((score - top) * SCALE).astype(BF16)
            values = jnp.concatenate([ref[tokens : 2 * tokens, :], ones], axis=1)
            total = total + dot(weights, values)
        mass = total[:, HD:]
        out_ref[here, :ITEM, :] = (total[:, :HD] / mass).astype(BF16).reshape(TILE, ITEM, HD)
        log_mass = to_lanes(top * SCALE + jnp.log2(mass), TILE)
        high = log_mass.astype(BF16).astype(F32)
        rest = log_mass - high
        middle = rest.astype(BF16).astype(F32)
        low = rest - middle
        shape = (TILE, STAT, HD)
        row = iota(shape, 1)
        stat = jnp.where(row == 0, jnp.broadcast_to(high[:, None, :], shape), 0.0)
        stat = jnp.where(row == 1, jnp.broadcast_to(middle[:, None, :], shape), stat)
        stat = jnp.where(row == 2, jnp.broadcast_to(low[:, None, :], shape), stat)
        out_ref[here, ITEM:, :] = stat.astype(BF16)


def combine_kernel(part_ref, own_ref, own_log_ref, out_ref):
    shards = part_ref.shape[0]
    log_mass = jnp.sum(part_ref[:, ITEM:, :].astype(F32), axis=1)
    own_log = own_log_ref[0:1, :]
    best = jnp.maximum(jnp.max(log_mass, axis=0, keepdims=True), own_log)
    weights = jnp.exp2(log_mass - best)
    own_weight = jnp.exp2(own_log - best)
    whole = jnp.sum(weights, axis=0, keepdims=True) + own_weight
    weights = weights / whole
    own_weight = own_weight / whole
    per_lane = HD // ITEM
    groups = shards // per_lane
    lane = iota((groups, HD), 1) // ITEM
    packed = jnp.zeros((groups, HD), F32)
    for turn in range(per_lane):
        packed = jnp.where(lane == turn, weights[turn * groups : (turn + 1) * groups], packed)
    pick = iota((ITEM, HD), 0) == iota((ITEM, HD), 1) % ITEM
    factors = []
    rows = []
    for group in range(groups):
        factors.append(jnp.where(pick, packed[group : group + 1], 0.0))
        for turn in range(per_lane):
            rows.append(part_ref[group + turn * groups, :ITEM, :])
    factor = jnp.concatenate(factors, axis=1)
    high = factor.astype(BF16)
    low = (factor - high.astype(F32)).astype(BF16)
    total = dot(jnp.concatenate([high, low], axis=0), jnp.concatenate(rows, axis=0))
    total = total[:ITEM] + total[ITEM:]
    own_column = jnp.sum(
        jnp.where(iota((ITEM, HD), 0) == iota((ITEM, HD), 1), own_weight, 0.0),
        axis=1,
        keepdims=True,
    )
    attended = (total + own_column * own_ref[...]).astype(BF16)
    out_ref[...] = jnp.broadcast_to(attended[None], out_ref.shape)


def peer_sample(peer):
    return peer * 11 % (SIDE * SIDE)


def project_kernel(x_ref, w_ref, out_ref, rows_ref):
    samples = x_ref.shape[0]
    parts = out_ref.shape[0]
    per_part = samples // parts
    for peer in range(samples):
        start = peer_sample(peer) * ITEM
        rows_ref[start : start + ITEM, :] = x_ref[peer].astype(F32)
    columns = []
    for head in range(PER):
        pieces = [
            rows_ref[pl.ds(step * PER + head, samples, stride=ITEM), :] for step in range(STEPS)
        ]
        columns.append(jnp.concatenate(pieces, axis=0).astype(BF16))
    product = dot(jnp.concatenate(columns, axis=1), w_ref[...])
    for part in range(parts):
        pieces = [
            product[step * samples + part * per_part : step * samples + (part + 1) * per_part]
            for step in range(STEPS)
        ]
        out_ref[part] = jnp.concatenate(pieces, axis=0).astype(out_ref.dtype)


def sum_kernel(x_ref, out_ref):
    total = jnp.sum(x_ref[...].astype(F32), axis=0)
    out_ref[...] = total.reshape(out_ref.shape).astype(BF16)


def call(
    kernel, name, out_shape, in_specs, out_specs, scratch=(), flops=0, moved=0, vmem=24
):
    return pl.pallas_call(
        kernel,
        name=name,
        out_shape=out_shape,
        in_specs=in_specs,
        out_specs=out_specs,
        scratch_shapes=scratch,
        compiler_params=pltpu.CompilerParams(vmem_limit_bytes=vmem * 1024 * 1024),
        cost_estimate=pl.CostEstimate(flops=flops, bytes_accessed=moved, transcendentals=0),
    )


def swap(array, axes, groups=None):
    return lax.all_to_all(
        array, axes, split_axis=0, concat_axis=0, axis_index_groups=groups, tiled=True
    )


def device(z, y, head):
    return (z % SIDE * SIDE + y % SIDE) * KVH + head


def far_groups():
    groups = []
    for head in range(KVH):
        for first in range(0, SIDE, GAP):
            group = []
            for ring in range(SIDE):
                for near in range(first, first + GAP):
                    z, y = (ring, near) if head % CORES == 0 else (near, ring)
                    group.append(device(z, y, head))
            groups.append(group)
    return groups


def all_groups():
    return [
        [peer_sample(peer) * KVH + head for peer in range(SIDE * SIDE)] for head in range(KVH)
    ]


def hops(count):
    pairs = []
    for head in range(KVH):
        for z in range(SIDE):
            for y in range(SIDE):
                move = count * GAP
                target = (z, y + move) if head % CORES == 0 else (z + move, y)
                pairs.append((device(z, y, head), device(*target, head)))
    return pairs


def shards(
    queries,
    prompt_keys,
    prompt_values,
    selected,
    cache_keys,
    cache_values,
    new_keys,
    new_values,
    positions,
    out_weight,
):
    struct = jax.ShapeDtypeStruct
    samples = lax.axis_size("ctx")
    far = SIDE * GAP
    heads = lax.axis_size("head")
    tokens = prompt_keys.shape[0]
    columns = out_weight.shape[1]
    ctx = lax.axis_index("ctx")
    odd = lax.axis_index("head") % CORES
    start = jnp.where(odd == 0, ctx % SIDE // GAP * GAP, ctx // SIDE // GAP * GAP * SIDE)
    place = (odd * (SIDE * SIDE) + start).astype(jnp.int32).reshape(1)
    groups = far_groups()
    rows_scratch = pltpu.VMEM((ITEM, HD), F32)
    q = queries.reshape(STEPS, PER * HD)

    chosen = selected[:, 0, :].T
    spread, here = call(
        pack_kernel,
        "pack",
        (struct((far, ITEM, HD), BF16), struct((2 * tokens + FLAG, HD), BF16)),
        [ANY] * 4,
        (VMEM, VMEM),
        [
            pltpu.VMEM(q.shape, BF16),
            pltpu.VMEM(chosen.shape, jnp.int32),
            rows_scratch,
            pltpu.SemaphoreType.DMA((4,)),
        ],
        vmem=62,
    )(q, prompt_keys, prompt_values, chosen)
    gathered = swap(spread, BOTH, groups)
    packs = [here]
    for count in range(1, SIDE // GAP):
        packs.append(lax.ppermute(here, BOTH, hops(count)))
    own, own_log = call(
        own_kernel,
        "own",
        (struct((ITEM, HD), F32), struct((8, HD), F32)),
        [VMEM] * 5 + [SMEM],
        (VMEM, VMEM),
        [rows_scratch],
        flops=10**6,
        moved=3 * 10**5,
    )(q, cache_keys[0], cache_values[0], new_keys[:, 0], new_values[:, 0], positions)
    partial = call(
        prompt_kernel,
        "prompt",
        struct((far, ITEM + STAT, HD), BF16),
        [SMEM, ANY] + [VMEM] * 5,
        VMEM,
        [pltpu.VMEM((2 * HD, 4 * tokens), BF16)],
    )(place, own, gathered, *packs)
    received = swap(partial, BOTH, groups)
    attended = call(
        combine_kernel, "combine", struct((samples, ITEM, HD), BF16), [VMEM] * 3, VMEM
    )(received, own, own_log)
    every = swap(attended, BOTH, all_groups())
    product = call(
        project_kernel,
        "project",
        struct((heads, STEPS * samples // heads, columns), F32),
        [VMEM] * 2,
        VMEM,
        [pltpu.VMEM((samples * ITEM, HD), F32)],
    )(every, out_weight)
    terms = swap(product, "head")
    return call(
        sum_kernel, "sum", struct((STEPS, samples // heads, columns), BF16), [VMEM], VMEM
    )(terms)


def solution(mesh):
    placed = (
        P(None, "ctx", "head"),
        P("ctx", "head"),
        P("ctx", "head"),
        P(None, "head", "ctx"),
        P("ctx", None, "head"),
        P("ctx", None, "head"),
        P(None, "ctx", "head"),
        P(None, "ctx", "head"),
        P("ctx"),
        P("head", "ctx"),
    )
    return jax.shard_map(
        shards, mesh=mesh, in_specs=placed, out_specs=P(None, "head", "ctx"), check_vma=False
    )
```

```python
import math

import jax
import jax.numpy as jnp
from jax import lax
from jax.experimental import pallas as pl
from jax.experimental.pallas import tpu as pltpu
from jax.sharding import PartitionSpec as P

HD = 128
KVH = 8
PER = 16
BLOCK = 64
STEPS = 2
ITEM = STEPS * PER
STAT = 8
FLAG = 16
NEGATIVE = -1e30
SCALE = math.log2(math.e) / math.sqrt(HD)
TILE = 4
BOTH = ("ctx", "head")
SIDE = 8
CORES = 2
GAP = 2

VMEM = pl.BlockSpec(memory_space=pltpu.VMEM)
SMEM = pl.BlockSpec(memory_space=pltpu.SMEM)
ANY = pl.BlockSpec(memory_space=pl.ANY)
F32 = jnp.float32
BF16 = jnp.bfloat16


def dot(a, b):
    return lax.dot_general(a, b, (((1,), (0,)), ((), ())), preferred_element_type=F32)


def dot_t(a, b):
    return lax.dot_general(a, b, (((1,), (1,)), ((), ())), preferred_element_type=F32)


def iota(shape, dim):
    return lax.broadcasted_iota(jnp.int32, shape, dim)


def item_rows(q_ref, rows_ref):
    whole = q_ref[...].astype(F32)
    for step in range(STEPS):
        for head in range(PER):
            row = step * PER + head
            rows_ref[row : row + 1, :] = whole[step : step + 1, head * HD : (head + 1) * HD]
    return rows_ref[...]


def to_lanes(column, count):
    shape = (count, ITEM, HD)
    pick = iota(shape, 1) == iota(shape, 2) % ITEM
    return jnp.sum(jnp.where(pick, column.reshape(shape), 0.0), axis=1)


def pack_kernel(
    q_hbm, k_hbm, v_hbm, sel_hbm, spread_ref, out_ref, q_ref, sel_ref, rows_ref, sems
):
    tokens = k_hbm.shape[0]
    copies = [
        pltpu.make_async_copy(q_hbm, q_ref, sems.at[0]),
        pltpu.make_async_copy(sel_hbm, sel_ref, sems.at[1]),
        pltpu.make_async_copy(k_hbm, out_ref.at[:tokens], sems.at[2]),
        pltpu.make_async_copy(v_hbm, out_ref.at[tokens : 2 * tokens], sems.at[3]),
    ]
    for copy in copies:
        copy.start()
    copies[0].wait()
    rows = item_rows(q_ref, rows_ref).astype(BF16)
    spread_ref[...] = jnp.broadcast_to(rows[None], spread_ref.shape)
    copies[1].wait()
    slots, samples = sel_ref.shape
    number = iota((FLAG, samples), 0)
    bias = jnp.full((FLAG, samples), NEGATIVE, F32)
    for slot in range(slots):
        bias = jnp.where(sel_ref[slot : slot + 1, :] == number, 0.0, bias)
    bias = jnp.concatenate([bias, jnp.zeros((FLAG, HD - samples), F32)], axis=1)
    out_ref[2 * tokens :, :] = bias.astype(BF16)
    for copy in copies[2:]:
        copy.wait()


def own_kernel(q_ref, ck_ref, cv_ref, nk_ref, nv_ref, pos_ref, out_ref, log_ref, rows_ref):
    rows = item_rows(q_ref, rows_ref)
    slots = ck_ref.shape[0]
    scores = dot_t(rows.astype(BF16), ck_ref[...]) * SCALE
    alive = iota((ITEM, slots), 1) < pos_ref[0]
    scores = jnp.where(alive, scores, NEGATIVE)
    top = jnp.max(scores, axis=1, keepdims=True)
    step = iota((ITEM, 1), 0) // PER
    new_scores = []
    for token in range(STEPS):
        key = nk_ref[token : token + 1, :].astype(F32)
        score = jnp.sum(rows * key, axis=1, keepdims=True) * SCALE
        score = jnp.where(step >= token, score, NEGATIVE)
        new_scores.append(score)
        top = jnp.maximum(top, score)
    weights = jnp.where(alive, jnp.exp2(scores - top), 0.0)
    mass = jnp.sum(weights, axis=1, keepdims=True)
    total = dot(weights.astype(BF16), cv_ref[...])
    for token in range(STEPS):
        weight = jnp.where(step >= token, jnp.exp2(new_scores[token] - top), 0.0)
        mass = mass + weight
        value = nv_ref[token : token + 1, :].astype(F32)
        total = total + weight.astype(BF16).astype(F32) * value
    out_ref[...] = total / mass
    log_mass = jnp.broadcast_to(top + jnp.log2(mass), (ITEM, HD))
    log_ref[...] = jnp.broadcast_to(to_lanes(log_mass, 1), log_ref.shape)


def prompt_kernel(place_ref, own_ref, q_ref, *refs):
    *pack_refs, out_ref, keys_ref = refs
    samples = q_ref.shape[0]
    tokens = (pack_refs[0].shape[0] - FLAG) // 2
    widen = iota((FLAG, tokens), 1) // BLOCK == iota((FLAG, tokens), 0)
    widen = widen.astype(F32).astype(BF16)
    for index, ref in enumerate(pack_refs):
        place = slice(index * tokens, (index + 1) * tokens)
        keys_ref[:HD, place] = ref[:tokens, :].T
        bias = lax.dot_general(
            ref[2 * tokens :, :], widen, (((0,), (0,)), ((), ())), preferred_element_type=F32
        )
        keys_ref[HD:, place] = bias.astype(BF16)
    ones = jnp.ones((tokens, HD), BF16)
    count = TILE * ITEM
    number = iota((count, HD), 0) // ITEM
    ring, near = number // GAP, number % GAP
    odd, start = place_ref[0] // (SIDE * SIDE), place_ref[0] % (SIDE * SIDE)
    sample = jnp.where(odd == 0, ring * SIDE + near, near * SIDE + ring)
    lane = iota((count, HD), 1) - sample
    for first in range(0, samples, TILE):
        here = slice(first, first + TILE)
        q = q_ref[here].reshape(count, HD)
        mine = lane == start + first // GAP * jnp.where(odd == 0, SIDE, 1)
        q = jnp.concatenate([q, mine.astype(F32).astype(BF16)], axis=1)
        scores = []
        for index in range(len(pack_refs)):
            scores.append(dot(q, keys_ref[:, index * tokens : (index + 1) * tokens]))
        top = scores[0]
        for score in scores[1:]:
            top = jnp.maximum(top, score)
        top = jnp.max(top, axis=1, keepdims=True)
        total = jnp.zeros((count, 2 * HD), F32)
        for score, ref in zip(scores, pack_refs):
            weights = jnp.exp2((score - top) * SCALE).astype(BF16)
            values = jnp.concatenate([ref[tokens : 2 * tokens, :], ones], axis=1)
            total = total + dot(weights, values)
        mass = total[:, HD:]
        out_ref[here, :ITEM, :] = (total[:, :HD] / mass).astype(BF16).reshape(TILE, ITEM, HD)
        log_mass = to_lanes(top * SCALE + jnp.log2(mass), TILE)
        high = log_mass.astype(BF16).astype(F32)
        rest = log_mass - high
        middle = rest.astype(BF16).astype(F32)
        low = rest - middle
        shape = (TILE, STAT, HD)
        row = iota(shape, 1)
        stat = jnp.where(row == 0, jnp.broadcast_to(high[:, None, :], shape), 0.0)
        stat = jnp.where(row == 1, jnp.broadcast_to(middle[:, None, :], shape), stat)
        stat = jnp.where(row == 2, jnp.broadcast_to(low[:, None, :], shape), stat)
        out_ref[here, ITEM:, :] = stat.astype(BF16)


def combine_kernel(part_ref, own_ref, own_log_ref, out_ref):
    shards = part_ref.shape[0]
    log_mass = jnp.sum(part_ref[:, ITEM:, :].astype(F32), axis=1)
    own_log = own_log_ref[0:1, :]
    best = jnp.maximum(jnp.max(log_mass, axis=0, keepdims=True), own_log)
    weights = jnp.exp2(log_mass - best)
    own_weight = jnp.exp2(own_log - best)
    whole = jnp.sum(weights, axis=0, keepdims=True) + own_weight
    weights = weights / whole
    own_weight = own_weight / whole
    per_lane = HD // ITEM
    groups = shards // per_lane
    lane = iota((groups, HD), 1) // ITEM
    packed = jnp.zeros((groups, HD), F32)
    for turn in range(per_lane):
        packed = jnp.where(lane == turn, weights[turn * groups : (turn + 1) * groups], packed)
    pick = iota((ITEM, HD), 0) == iota((ITEM, HD), 1) % ITEM
    factors = []
    rows = []
    for group in range(groups):
        factors.append(jnp.where(pick, packed[group : group + 1], 0.0))
        for turn in range(per_lane):
            rows.append(part_ref[group + turn * groups, :ITEM, :])
    factor = jnp.concatenate(factors, axis=1)
    high = factor.astype(BF16)
    low = (factor - high.astype(F32)).astype(BF16)
    total = dot(jnp.concatenate([high, low], axis=0), jnp.concatenate(rows, axis=0))
    total = total[:ITEM] + total[ITEM:]
    own_column = jnp.sum(
        jnp.where(iota((ITEM, HD), 0) == iota((ITEM, HD), 1), own_weight, 0.0),
        axis=1,
        keepdims=True,
    )
    attended = (total + own_column * own_ref[...]).astype(BF16)
    out_ref[...] = jnp.broadcast_to(attended[None], out_ref.shape)


def peer_sample(peer):
    return peer * 11 % (SIDE * SIDE)


def project_kernel(x_ref, w_ref, out_ref, rows_ref):
    samples = x_ref.shape[0]
    parts = out_ref.shape[0]
    per_part = samples // parts
    for peer in range(samples):
        start = peer_sample(peer) * ITEM
        rows_ref[start : start + ITEM, :] = x_ref[peer].astype(F32)
    columns = []
    for head in range(PER):
        pieces = [
            rows_ref[pl.ds(step * PER + head, samples, stride=ITEM), :] for step in range(STEPS)
        ]
        columns.append(jnp.concatenate(pieces, axis=0).astype(BF16))
    product = dot(jnp.concatenate(columns, axis=1), w_ref[...])
    for part in range(parts):
        pieces = [
            product[step * samples + part * per_part : step * samples + (part + 1) * per_part]
            for step in range(STEPS)
        ]
        out_ref[part] = jnp.concatenate(pieces, axis=0).astype(out_ref.dtype)


def sum_kernel(x_ref, out_ref):
    total = jnp.sum(x_ref[...].astype(F32), axis=0)
    out_ref[...] = total.reshape(out_ref.shape).astype(BF16)


def call(
    kernel, name, out_shape, in_specs, out_specs, scratch=(), flops=0, moved=0, vmem=24
):
    return pl.pallas_call(
        kernel,
        name=name,
        out_shape=out_shape,
        in_specs=in_specs,
        out_specs=out_specs,
        scratch_shapes=scratch,
        compiler_params=pltpu.CompilerParams(vmem_limit_bytes=vmem * 1024 * 1024),
        cost_estimate=pl.CostEstimate(flops=flops, bytes_accessed=moved, transcendentals=0),
    )


def swap(array, axes, groups=None):
    return lax.all_to_all(
        array, axes, split_axis=0, concat_axis=0, axis_index_groups=groups, tiled=True
    )


def device(z, y, head):
    return (z % SIDE * SIDE + y % SIDE) * KVH + head


def far_groups():
    groups = []
    for head in range(KVH):
        for first in range(0, SIDE, GAP):
            group = []
            for ring in range(SIDE):
                for near in range(first, first + GAP):
                    z, y = (ring, near) if head % CORES == 0 else (near, ring)
                    group.append(device(z, y, head))
            groups.append(group)
    return groups


def all_groups():
    return [
        [peer_sample(peer) * KVH + head for peer in range(SIDE * SIDE)] for head in range(KVH)
    ]


def hops(count):
    pairs = []
    for head in range(KVH):
        for z in range(SIDE):
            for y in range(SIDE):
                move = count * GAP
                target = (z, y + move) if head % CORES == 0 else (z + move, y)
                pairs.append((device(z, y, head), device(*target, head)))
    return pairs


def shards(
    queries,
    prompt_keys,
    prompt_values,
    selected,
    cache_keys,
    cache_values,
    new_keys,
    new_values,
    positions,
    out_weight,
):
    struct = jax.ShapeDtypeStruct
    samples = lax.axis_size("ctx")
    far = SIDE * GAP
    heads = lax.axis_size("head")
    tokens = prompt_keys.shape[0]
    columns = out_weight.shape[1]
    ctx = lax.axis_index("ctx")
    odd = lax.axis_index("head") % CORES
    start = jnp.where(odd == 0, ctx % SIDE // GAP * GAP, ctx // SIDE // GAP * GAP * SIDE)
    place = (odd * (SIDE * SIDE) + start).astype(jnp.int32).reshape(1)
    groups = far_groups()
    rows_scratch = pltpu.VMEM((ITEM, HD), F32)
    q = queries.reshape(STEPS, PER * HD)

    chosen = selected[:, 0, :].T
    spread, here = call(
        pack_kernel,
        "pack",
        (struct((far, ITEM, HD), BF16), struct((2 * tokens + FLAG, HD), BF16)),
        [ANY] * 4,
        (VMEM, VMEM),
        [
            pltpu.VMEM(q.shape, BF16),
            pltpu.VMEM(chosen.shape, jnp.int32),
            rows_scratch,
            pltpu.SemaphoreType.DMA((4,)),
        ],
        vmem=62,
    )(q, prompt_keys, prompt_values, chosen)
    gathered = swap(spread, BOTH, groups)
    packs = [here]
    for count in range(1, SIDE // GAP):
        packs.append(lax.ppermute(here, BOTH, hops(count)))
    own, own_log = call(
        own_kernel,
        "own",
        (struct((ITEM, HD), F32), struct((8, HD), F32)),
        [VMEM] * 5 + [SMEM],
        (VMEM, VMEM),
        [rows_scratch],
        flops=10**6,
        moved=3 * 10**5,
    )(q, cache_keys[0], cache_values[0], new_keys[:, 0], new_values[:, 0], positions)
    partial = call(
        prompt_kernel,
        "prompt",
        struct((far, ITEM + STAT, HD), BF16),
        [SMEM, ANY] + [VMEM] * 5,
        VMEM,
        [pltpu.VMEM((2 * HD, 4 * tokens), BF16)],
    )(place, own, gathered, *packs)
    received = swap(partial, BOTH, groups)
    attended = call(
        combine_kernel, "combine", struct((samples, ITEM, HD), BF16), [VMEM] * 3, VMEM
    )(received, own, own_log)
    every = swap(attended, BOTH, all_groups())
    product = call(
        project_kernel,
        "project",
        struct((heads, STEPS * samples // heads, columns), BF16),
        [VMEM] * 2,
        VMEM,
        [pltpu.VMEM((samples * ITEM, HD), F32)],
    )(every, out_weight)
    terms = swap(product, "head")
    return call(
        sum_kernel, "sum", struct((STEPS, samples // heads, columns), BF16), [VMEM], VMEM
    )(terms)


def solution(mesh):
    placed = (
        P(None, "ctx", "head"),
        P("ctx", "head"),
        P("ctx", "head"),
        P(None, "head", "ctx"),
        P("ctx", None, "head"),
        P("ctx", None, "head"),
        P(None, "ctx", "head"),
        P(None, "ctx", "head"),
        P("ctx"),
        P("head", "ctx"),
    )
    return jax.shard_map(
        shards, mesh=mesh, in_specs=placed, out_specs=P(None, "head", "ctx"), check_vma=False
    )
```
